32 devices in a mesh: groups: 2 (over x), rows: 16 (over z, y, core).
Axes of the slice: x: 2, y: 2, z: 4, core: 2. Of those that a mesh axis runs over, the one named last changes fastest.
Arguments:
- embeddings: bfloat16 [49152, 1024], P(('groups', 'rows')), parts along dimension 0
- block_cluster: int32 [384], P('groups'), parts along dimension 0, may hold values from 0 to 191, as said below
- pair_blocks: int32 [6720, 2], P(('groups', 'rows')), parts along dimension 0, may hold values from 0 to 191, as said below
Outputs:
- best_match: float32 [49152], P(('groups', 'rows')), parts along dimension 0
The draws below stay inside these ranges and needn't reach their ends.
There are 2 independent parts, one for each index of `groups`. The reference program is written for one: setup_inputs(seed, part) draws one part's arguments, and reference() takes and returns one part's arrays. A program takes and returns all parts, laid end to end along the dimension named above; each array names one. Nothing has to cross between parts.
Inputs may be any that keep to these rules, and one draw needn't show every extreme that they name: `block_cluster`: every cluster is a run of consecutive blocks, at most 24 long; different clusters have different ids. `pair_blocks`: slots 210 * i to 210 * i + 209 belong to device i of rows. Each slot (a, b) has block a on that device and a <= b; the slots with a < b name each pair a < b of same-cluster blocks whose a lies on that device exactly once; the other slots have a == b.
All inputs are finite; a program needn't handle non-finite values.
Results may differ from the reference program's by a relative error of at most 0.0011.
Values may be sent and summed in bfloat16 or wider, within the bound.
No kernel may reach another device: no remote copies, remote signals or barrier semaphores. Data moves between devices by JAX's collectives and lax.ppermute only.
A program may use at most 64 MiB of HBM per device.

```python
import jax
import jax.numpy as jnp
from jax import lax

D = 1024
BLOCK = 128
BLOCKS_DEV = 12
LMAX = 24
SLOTS = 210
NBLOCKS = 192
ROWS_ALL = 24576


def cluster_layout(key):
    key_big, key_long, key_short = jax.random.split(key, 3)
    chosen_big = jax.random.randint(key_big, (NBLOCKS,), 0, 2) == 0
    long_length = LMAX - jax.random.randint(key_long, (NBLOCKS,), 0, 3)
    short_length = jax.random.randint(key_short, (NBLOCKS,), 1, 5)
    position = jnp.arange(NBLOCKS, dtype=jnp.int32)
    lengths = jnp.where(chosen_big, long_length, short_length)
    lengths = jnp.where(position == 0, BLOCKS_DEV - 1, jnp.where(position == 1, LMAX, lengths))
    starts = jnp.cumsum(lengths) - lengths
    layout = jnp.searchsorted(starts, position, side='right') - 1
    end_ids = jnp.minimum(starts + lengths - 1, NBLOCKS - 1)
    return (starts[layout].astype(jnp.int32), end_ids[layout].astype(jnp.int32))


def draw_block_cluster(key, part):
    starts, end_ids = cluster_layout(key)
    return end_ids


def draw_pair_blocks(key, part):
    starts, layout = cluster_layout(key)
    devices = NBLOCKS // BLOCKS_DEV
    owner_first = jnp.arange(devices, dtype=jnp.int32) * BLOCKS_DEV
    left_ids = owner_first[:, None] + jnp.repeat(jnp.arange(BLOCKS_DEV, dtype=jnp.int32), LMAX - 1)[None, :]
    right_ids = left_ids + jnp.tile(jnp.arange(1, LMAX, dtype=jnp.int32), BLOCKS_DEV)[None, :]
    inside = right_ids < NBLOCKS
    clipped = jnp.minimum(right_ids, NBLOCKS - 1)
    counted = inside & (layout[clipped] == layout[left_ids])
    filler = (owner_first + BLOCKS_DEV - 1)[:, None] * jnp.ones((1, SLOTS), jnp.int32)
    left_ids = jnp.concatenate([left_ids, filler], axis=1)
    right_ids = jnp.concatenate([right_ids, filler], axis=1)
    counted = jnp.concatenate([counted, jnp.zeros((devices, SLOTS), bool)], axis=1)
    ranking = jnp.argsort(jnp.where(counted, 0, 1), axis=1, stable=True)[:, :SLOTS]
    picked = jnp.take_along_axis(counted, ranking, axis=1)
    left_pick = jnp.where(picked, jnp.take_along_axis(left_ids, ranking, axis=1), filler)
    right_pick = jnp.where(picked, jnp.take_along_axis(right_ids, ranking, axis=1), filler)
    return jnp.stack([left_pick, right_pick], axis=-1).reshape(-1, 2).astype(jnp.int32)


def draw_embeddings(key, part):
    starts, end_ids = cluster_layout(key)
    key = jax.random.fold_in(key, 5)
    key_centre, key_weight, key_order, key_flip, key_step, key_coin, key_rank, key_noise, key_fresh, key_tight = jax.random.split(key, 10)
    centres = jax.random.normal(key_centre, (NBLOCKS, D), jnp.float32)
    block_of_row = jnp.arange(ROWS_ALL, dtype=jnp.int32) // BLOCK
    weights = jax.random.uniform(key_weight, (ROWS_ALL, 1), jnp.float32, 0.04, 0.16)
    order_scores = jax.random.randint(key_order, (NBLOCKS, BLOCK), 0, 1 << 20) * BLOCK + jnp.arange(BLOCK, dtype=jnp.int32)[None, :]
    row_order = jnp.argsort(order_scores, axis=1).astype(jnp.int32)
    rank_in_block = jnp.argsort(row_order, axis=1).reshape(-1).astype(jnp.int32)
    row_start = starts[block_of_row]
    length = end_ids[block_of_row] - row_start + 1
    within = block_of_row - row_start
    flip_draw = jax.random.randint(key_flip, (ROWS_ALL,), 0, 3)
    duplicate = (rank_in_block < BLOCK // 2) & ((rank_in_block == 0) | (flip_draw < 2)) & (length > 1)
    mirror = length - 1 - within
    mirror = jnp.where(mirror == within, (within + 1) % length, mirror)
    step_draw = jax.random.randint(key_step, (ROWS_ALL,), 0, LMAX)
    random_other = (within + 1 + step_draw % jnp.maximum(length - 1, 1)) % length
    coin_draw = jax.random.randint(key_coin, (ROWS_ALL,), 0, 2)
    companion_block = row_start + jnp.where((rank_in_block == 0) | (coin_draw == 0), mirror, random_other)
    companion_position = BLOCK // 2 + jax.random.randint(key_rank, (ROWS_ALL,), 0, BLOCK - BLOCK // 2)
    partner_row = companion_block * BLOCK + row_order.reshape(-1)[companion_block * BLOCK + companion_position]
    tightness = jax.random.uniform(key_tight, (ROWS_ALL, 1), jnp.float32, 0.15, 0.45)
    noise_rows = jax.random.normal(key_noise, (ROWS_ALL, D), jnp.float32)
    fresh_noise = jax.random.normal(key_fresh, (ROWS_ALL, D), jnp.float32)
    base_rows = weights * centres[end_ids[block_of_row]] + noise_rows
    partner_weight = weights[partner_row]
    copied = base_rows[partner_row] + tightness * jnp.sqrt(partner_weight * partner_weight + 1.0) * fresh_noise
    values = jnp.where(duplicate[:, None], copied, base_rows)
    return values.astype(jnp.bfloat16)


def setup_inputs(seed: int = 0, part: int = 0) -> dict:
    key_of = jax.random.split(jax.random.key(seed), 4)
    part_keys = jax.random.split(jax.random.fold_in(key_of[3], part), 4)
    embeddings = draw_embeddings(jax.random.fold_in(jax.random.fold_in(key_of[3], part), 71), part)
    block_cluster = draw_block_cluster(jax.random.fold_in(jax.random.fold_in(key_of[3], part), 71), part)
    pair_blocks = draw_pair_blocks(jax.random.fold_in(jax.random.fold_in(key_of[3], part), 71), part)
    return {"embeddings": embeddings, "block_cluster": block_cluster, "pair_blocks": pair_blocks}


def reference(embeddings, block_cluster, pair_blocks):
    broadened_rows = embeddings.astype(jnp.float32)
    unit_rows = (broadened_rows * lax.rsqrt(lax.optimization_barrier(jnp.sum(broadened_rows * broadened_rows, axis=1, keepdims=True)) + 1e-06)).astype(jnp.bfloat16)
    blocks = unit_rows.reshape(-1, BLOCK, D)
    diagonal_mask = jnp.eye(BLOCK, dtype=bool)

    def own_block(single):
        products = jnp.dot(single, single.T, preferred_element_type=jnp.float32)
        products = jnp.where(diagonal_mask, jnp.float32(-3.0), products)
        return lax.optimization_barrier(jnp.max(products, axis=1))
    best_rows = lax.map(own_block, blocks)

    def visit_slot(best_rows, pair_ids):
        left_id = pair_ids[0]
        right_id = pair_ids[1]
        counted = (left_id != right_id) & (block_cluster[left_id] == block_cluster[right_id])

        def add_tile(current):
            products = jnp.dot(blocks[left_id], blocks[right_id].T, preferred_element_type=jnp.float32)
            current = current.at[left_id].max(lax.optimization_barrier(jnp.max(products, axis=1)))
            return current.at[right_id].max(lax.optimization_barrier(jnp.max(products, axis=0)))
        return (lax.cond(counted, add_tile, lambda current: current, best_rows), None)
    best_rows, _ = lax.scan(visit_slot, best_rows, pair_blocks)
    return best_rows.reshape(-1)
```

```python
import functools

import jax
import jax.numpy as jnp
from jax import lax
from jax.experimental import pallas as pl
from jax.experimental.pallas import tpu as pltpu
from jax.sharding import PartitionSpec as P

BLOCK = 128
NEVER = -3.0
MIB = 1 << 20
FAR_AWAY = 1 << 20
SMEM = pltpu.SMEM
VMEM = pltpu.VMEM


def plan_kernel(chip_blocks, cluster_ref, plan_ref, left_part, right_part, from_left, turn):
    here = chip_blocks // 2
    chips = cluster_ref.shape[0] // chip_blocks
    me = lax.axis_index("rows")

    def run_length(start, step):
        count = jnp.int32(0)
        for jump in (16, 8, 4, 2, 1):
            further = count + jump
            same = cluster_ref[start + step * further] == cluster_ref[start]
            count = jnp.where(same, further, count)
        return count

    def cost(blocks):
        return jnp.where(blocks > here, FAR_AWAY, blocks)

    def forward(boundary, carry):
        best_left, best_right, load_right = carry
        edge = (boundary + 1) * chip_blocks
        behind = run_length(edge, -1)
        ahead = run_length(edge - 1, 1)
        left_part[boundary] = behind
        right_part[boundary] = ahead
        by_left = jnp.maximum(best_left, cost(ahead))
        by_right = jnp.maximum(best_right, load_right + cost(ahead))
        from_left[boundary] = jnp.where(by_left <= by_right, 0, 1)
        stays_right = jnp.maximum(best_right, load_right)
        from_left[chips + boundary] = jnp.where(best_left <= stays_right, 0, 1)
        return jnp.minimum(by_left, by_right), jnp.minimum(best_left, stays_right), cost(behind)

    best_left, best_right, load_right = lax.fori_loop(
        0, chips - 1, forward, (jnp.int32(0), jnp.int32(FAR_AWAY), jnp.int32(0))
    )
    last = jnp.where(best_left <= jnp.maximum(best_right, load_right), 0, 1)

    def backward(step, state):
        boundary = chips - 2 - step
        turn[boundary] = state
        return from_left[state * chips + boundary]

    lax.fori_loop(0, chips - 1, backward, last)
    upper = lax.rem(me, 2)
    mine = lax.div(me, 2) - 1 + upper
    inside = (mine >= 0) & (mine < chips - 1)
    mine = jnp.clip(mine, 0, chips - 2)
    behind, ahead, rightwards = left_part[mine], right_part[mine], turn[mine]
    live = inside & (behind > 0) & (ahead > 0)
    receives = live & (rightwards != upper)
    sent = jnp.where(rightwards == 1, behind, ahead)
    paired = jnp.where(rightwards == 1, ahead, behind)
    plan_ref[0] = jnp.where(live, 1 + rightwards, 0)
    plan_ref[1] = jnp.where(receives, sent, 0)
    plan_ref[2] = jnp.where(receives, jnp.minimum(paired, here), 0)
    plan_ref[3] = jnp.where(receives, jnp.maximum(paired - here, 0), 0)
    plan_ref[4] = upper
    plan_ref[5] = me * here
    plan_ref[6] = (me + 1 - 2 * upper) * here
    plan_ref[7] = jnp.where(live & (rightwards == upper), sent, 0)


def make_plan(block_cluster, chip_blocks):
    chips = block_cluster.shape[0] // chip_blocks
    return pl.pallas_call(
        functools.partial(plan_kernel, chip_blocks),
        out_shape=jax.ShapeDtypeStruct((8,), jnp.int32),
        in_specs=[pl.BlockSpec(memory_space=SMEM)],
        out_specs=pl.BlockSpec(memory_space=SMEM),
        scratch_shapes=[
            SMEM((chips,), jnp.int32),
            SMEM((chips,), jnp.int32),
            SMEM((2 * chips,), jnp.int32),
            SMEM((chips,), jnp.int32),
        ],
    )(block_cluster)


def unit(rows):
    broadened = rows.astype(jnp.float32)
    total = jnp.sum(broadened * broadened, axis=1, keepdims=True)
    return (broadened * lax.rsqrt(total + 1e-06)).astype(jnp.bfloat16)


def products(left, right):
    return lax.dot_general(
        left, right, (((1,), (1,)), ((), ())), preferred_element_type=jnp.float32
    )


def local_kernel(same_device, cluster_ref, plan_ref, rows_ref, own_ref, best_ref):
    blocks = own_ref.shape[0] // BLOCK
    own_first = plan_ref[5]
    rows_first = plan_ref[5] if same_device else plan_ref[6]
    tall, wide = 4, 2

    def tile(turn, _):
        best = [jnp.full((1, BLOCK), NEVER, jnp.float32) for _ in range(wide)]
        own_rows = own_ref[pl.ds(pl.multiple_of(turn * wide * BLOCK, wide * BLOCK), wide * BLOCK), :]
        for part in range(blocks // tall):
            product = products(rows_ref[part * tall * BLOCK : (part + 1) * tall * BLOCK, :], own_rows)
            if same_device:
                row = lax.broadcasted_iota(jnp.int32, product.shape, 0) + part * tall * BLOCK
                column = lax.broadcasted_iota(jnp.int32, product.shape, 1) + turn * wide * BLOCK
                product = jnp.where(row == column, NEVER, product)
            for i in range(tall):
                for j in range(wide):
                    same = (
                        cluster_ref[rows_first + part * tall + i]
                        == cluster_ref[own_first + turn * wide + j]
                    )
                    piece = product[i * BLOCK : (i + 1) * BLOCK, j * BLOCK : (j + 1) * BLOCK]
                    top = jnp.max(piece, axis=0, keepdims=True)
                    best[j] = jnp.maximum(best[j], jnp.where(same, top, NEVER))
        for j in range(wide):
            best_ref[pl.ds(turn * wide + j, 1), :] = best[j]
        return 0

    lax.fori_loop(0, blocks // wide, tile, 0)


def local_best(same_device, block_cluster, plan, rows, own):
    blocks = own.shape[0] // BLOCK
    flops = 2 * rows.shape[0] * own.shape[0] * own.shape[1]
    return pl.pallas_call(
        functools.partial(local_kernel, same_device),
        out_shape=jax.ShapeDtypeStruct((blocks, BLOCK), jnp.float32),
        in_specs=[pl.BlockSpec(memory_space=SMEM)] * 2 + [pl.BlockSpec(memory_space=VMEM)] * 2,
        out_specs=pl.BlockSpec(memory_space=VMEM),
        compiler_params=pltpu.CompilerParams(vmem_limit_bytes=24 * MIB),
        cost_estimate=pl.CostEstimate(flops=flops, bytes_accessed=4 * rows.size, transcendentals=0),
    )(block_cluster, plan, rows, own)


def cross_kernel(plan_ref, got_ref, own_ref, other_ref, back_ref, own_best_ref, other_best_ref, rows, row_best):
    blocks = got_ref.shape[0] // BLOCK
    count, near, far, upper = plan_ref[1], plan_ref[2], plan_ref[3], plan_ref[4]
    tall, wide = 4, 2
    back_ref[...] = jnp.full(back_ref.shape, NEVER, jnp.float32)
    own_best_ref[...] = jnp.full(own_best_ref.shape, NEVER, jnp.float32)
    other_best_ref[...] = jnp.full(other_best_ref.shape, NEVER, jnp.float32)
    got_from = jnp.where(upper == 1, 0, blocks - count)
    got_to = got_from + count

    def against(side_ref, best_ref, part, lowest, highest):
        def tile(turn, _):
            side = side_ref[pl.ds(pl.multiple_of(turn * wide * BLOCK, wide * BLOCK), wide * BLOCK), :]
            product = products(rows[...], side)
            best = [jnp.full((1, BLOCK), NEVER, jnp.float32) for _ in range(wide)]
            for j in range(wide):
                block = turn * wide + j
                fits = (block >= lowest) & (block < highest)
                for i in range(tall):
                    piece = product[i * BLOCK : (i + 1) * BLOCK, j * BLOCK : (j + 1) * BLOCK]
                    held = row_best[i * BLOCK : (i + 1) * BLOCK, :]
                    row_best[i * BLOCK : (i + 1) * BLOCK, :] = jnp.maximum(
                        held, jnp.where(fits, piece, NEVER)
                    )
                    valid = (part * tall + i >= got_from) & (part * tall + i < got_to) & fits
                    top = jnp.max(piece, axis=0, keepdims=True)
                    best[j] = jnp.maximum(best[j], jnp.where(valid, top, NEVER))
                at = pl.ds(block, 1)
                best_ref[at, :] = jnp.maximum(best_ref[at, :], best[j])
            return 0

        lax.fori_loop(lax.div(lowest, wide), lax.div(highest + wide - 1, wide), tile, 0)

    def chunk(part, _):
        start = pl.multiple_of(part * tall * BLOCK, tall * BLOCK)
        rows[...] = unit(got_ref[pl.ds(start, tall * BLOCK), :])
        row_best[...] = jnp.full(row_best.shape, NEVER, jnp.float32)
        near_from = jnp.where(upper == 1, blocks - near, 0)
        against(own_ref, own_best_ref, part, near_from, near_from + near)
        far_from = jnp.where(upper == 1, blocks - far, 0)
        against(other_ref, other_best_ref, part, far_from, far_from + far)
        for i in range(tall):
            block = part * tall + i
            valid = (block >= got_from) & (block < got_to)
            top = jnp.max(row_best[i * BLOCK : (i + 1) * BLOCK, :].T, axis=0, keepdims=True)
            back_ref[pl.ds(block, 1), :] = jnp.where(valid, top, NEVER)
        return 0

    lax.fori_loop(lax.div(got_from, tall), lax.div(got_to + tall - 1, tall), chunk, 0)


def cross_best(plan, got, own, other):
    blocks = own.shape[0] // BLOCK
    features = own.shape[1]
    out = jax.ShapeDtypeStruct((blocks, BLOCK), jnp.float32)
    vmem = pl.BlockSpec(memory_space=VMEM)
    return pl.pallas_call(
        cross_kernel,
        out_shape=(out, out, out),
        in_specs=[pl.BlockSpec(memory_space=SMEM)] + [vmem] * 3,
        out_specs=(vmem, vmem, vmem),
        scratch_shapes=[VMEM((4 * BLOCK, features), jnp.bfloat16), VMEM((4 * BLOCK, BLOCK), jnp.float32)],
        compiler_params=pltpu.CompilerParams(vmem_limit_bytes=24 * MIB),
        cost_estimate=pl.CostEstimate(
            flops=2 * own.shape[0] * own.shape[0] * features, bytes_accessed=6 * own.size, transcendentals=0
        ),
    )(plan, got, own, other)


def on_device(embeddings, block_cluster, pair_blocks):
    blocks = embeddings.shape[0] // BLOCK
    devices = lax.axis_size("rows")
    swap = [(i, i ^ 1) for i in range(devices)]
    leftwards = [(i + 1, i) for i in range(1, devices - 1, 2)]
    rightwards = [(b, a) for a, b in leftwards]

    plan = make_plan(block_cluster, 2 * blocks)
    own = unit(embeddings)
    other = lax.ppermute(own, "rows", swap)

    def send(route):
        def branch(embeddings, own):
            got = lax.ppermute(embeddings, "rows", route)
            return got, local_best(True, block_cluster, plan, own, own)

        return branch

    def stay(embeddings, own):
        return embeddings, local_best(True, block_cluster, plan, own, own)

    got, best = lax.switch(plan[0], [stay, send(leftwards), send(rightwards)], embeddings, own)
    back, own_best, other_best = cross_best(plan, got, own, other)

    def answer(route):
        def branch(back, own, other):
            returned = lax.ppermute(back, "rows", route)
            return returned, local_best(False, block_cluster, plan, other, own)

        return branch

    def silent(back, own, other):
        return back, local_best(False, block_cluster, plan, other, own)

    returned, beside = lax.switch(
        plan[0], [silent, answer(rightwards), answer(leftwards)], back, own, other
    )
    from_core = lax.ppermute(other_best, "rows", swap)
    best = jnp.maximum(jnp.maximum(best, beside), jnp.maximum(own_best, from_core))
    best = jnp.where(plan[7] > 0, jnp.maximum(best, returned), best)
    return best.reshape(-1)


def solution(mesh):
    placed = (P(("groups", "rows"), None), P("groups"), P(("groups", "rows"), None))
    return jax.shard_map(
        on_device, mesh=mesh, in_specs=placed, out_specs=P(("groups", "rows")), check_vma=False
    )
```

```python
import functools

import jax
import jax.numpy as jnp
from jax import lax
from jax.experimental import pallas as pl
from jax.experimental.pallas import tpu as pltpu
from jax.sharding import PartitionSpec as P

BLOCK = 128
NEVER = -3.0
MIB = 1 << 20
FAR_AWAY = 1 << 20
EARLY = 2
LEFT_SIZES = (2, 8, 11, 12)
LEFT_PIECES = ((), (6,), (6, 3), (6, 4))
RIGHT_SIZES = (4, 8, 12)
RIGHT_PIECES = ((4,), (4, 4), (8, 4))
SMEM = pltpu.SMEM
VMEM = pltpu.VMEM


def plan_kernel(chip_blocks, cluster_ref, way_ref, turn_ref, plan_ref, left_part, right_part, from_left, turn):
    here = chip_blocks // 2
    chips = cluster_ref.shape[0] // chip_blocks
    me = lax.axis_index("rows")

    def run_length(start, step):
        count = jnp.int32(0)
        for jump in (16, 8, 4, 2, 1):
            further = count + jump
            same = cluster_ref[start + step * further] == cluster_ref[start]
            count = jnp.where(same, further, count)
        return count

    def cost(blocks):
        return jnp.where(blocks > here, FAR_AWAY, blocks)

    def forward(boundary, carry):
        best_left, best_right, load_right = carry
        edge = (boundary + 1) * chip_blocks
        behind = run_length(edge, -1)
        ahead = run_length(edge - 1, 1)
        left_part[boundary] = behind
        right_part[boundary] = ahead
        leftwards = jnp.where(ahead > here, FAR_AWAY, jnp.maximum(ahead - EARLY, 0))
        by_left = jnp.maximum(best_left, leftwards)
        by_right = jnp.maximum(best_right, load_right + leftwards)
        from_left[boundary] = jnp.where(by_left <= by_right, 0, 1)
        stays_right = jnp.maximum(best_right, load_right)
        from_left[chips + boundary] = jnp.where(best_left <= stays_right, 0, 1)
        return jnp.minimum(by_left, by_right), jnp.minimum(best_left, stays_right), cost(behind)

    best_left, best_right, load_right = lax.fori_loop(
        0, chips - 1, forward, (jnp.int32(0), jnp.int32(FAR_AWAY), jnp.int32(0))
    )
    last = jnp.where(best_left <= jnp.maximum(best_right, load_right), 0, 1)

    def backward(step, state):
        boundary = chips - 2 - step
        turn[boundary] = state
        return from_left[state * chips + boundary]

    lax.fori_loop(0, chips - 1, backward, last)
    upper = lax.rem(me, 2)
    mine = lax.div(me, 2) - 1 + upper
    inside = (mine >= 0) & (mine < chips - 1)
    mine = jnp.clip(mine, 0, chips - 2)
    behind, ahead, rightwards = left_part[mine], right_part[mine], turn[mine]
    live = inside & (behind > 0) & (ahead > 0)
    receives = live & (rightwards != upper)
    sent = jnp.where(rightwards == 1, behind, ahead)
    paired = jnp.where(rightwards == 1, ahead, behind)
    middle = lax.div(me, 2) * chip_blocks + here
    below = jnp.minimum(run_length(middle, -1), here)
    above = jnp.minimum(run_length(middle - 1, 1), here)
    left_size, right_size = jnp.int32(1), jnp.int32(1 + len(LEFT_SIZES))
    for bound in LEFT_SIZES[:-1]:
        left_size = left_size + (sent > bound).astype(jnp.int32)
    for bound in RIGHT_SIZES[:-1]:
        right_size = right_size + (sent > bound).astype(jnp.int32)
    size = jnp.where(rightwards == 1, right_size, left_size)
    way_ref[0] = jnp.where(live, size, 0)
    turn_ref[0] = jnp.where(live, 1 + rightwards, 0)
    plan_ref[0] = (live & (rightwards == upper)).astype(jnp.int32)
    plan_ref[1] = jnp.where(receives, sent, 0)
    plan_ref[2] = jnp.where(receives, jnp.minimum(paired, here), 0)
    plan_ref[3] = jnp.where(receives, jnp.maximum(paired - here, 0), 0)
    plan_ref[4] = upper
    plan_ref[5] = me * here
    plan_ref[6] = jnp.where(upper == 1, above, below)
    plan_ref[7] = jnp.where(upper == 1, below, above)


def make_plan(block_cluster, chip_blocks):
    chips = block_cluster.shape[0] // chip_blocks
    return pl.pallas_call(
        functools.partial(plan_kernel, chip_blocks),
        out_shape=tuple(jax.ShapeDtypeStruct((n,), jnp.int32) for n in (1, 1, 8)),
        in_specs=[pl.BlockSpec(memory_space=SMEM)],
        out_specs=(pl.BlockSpec(memory_space=SMEM),) * 3,
        scratch_shapes=[
            SMEM((chips,), jnp.int32),
            SMEM((chips,), jnp.int32),
            SMEM((2 * chips,), jnp.int32),
            SMEM((chips,), jnp.int32),
        ],
    )(block_cluster)


def unit(rows):
    broadened = rows.astype(jnp.float32)
    total = jnp.sum(broadened * broadened, axis=1, keepdims=True)
    return (broadened * lax.rsqrt(total + 1e-06)).astype(jnp.bfloat16)


def products(left, right):
    return lax.dot_general(
        left, right, (((1,), (1,)), ((), ())), preferred_element_type=jnp.float32
    )


def local_kernel(cluster_ref, plan_ref, rows_ref, other_ref, chip_ref, best_ref):
    blocks = rows_ref.shape[0] // BLOCK
    upper, first, theirs = plan_ref[4], plan_ref[5], plan_ref[7]
    tall, wide = 4, 2
    size = wide * BLOCK

    def normalise(turn, _):
        at = pl.ds(pl.multiple_of(turn * size, size), size)
        chip_ref[at, :] = unit(rows_ref[at, :])
        return 0

    lax.fori_loop(0, blocks // wide, normalise, 0)

    def normalise_other(turn, _):
        start = pl.multiple_of(turn * size, size)
        chip_ref[pl.ds(start + blocks * BLOCK, size), :] = unit(other_ref[pl.ds(start, size), :])
        return 0

    their_from = jnp.where(upper == 1, blocks - theirs, 0)
    their_tiles = lax.div(their_from, wide), lax.div(their_from + theirs + wide - 1, wide)
    lax.fori_loop(their_tiles[0], their_tiles[1], normalise_other, 0)
    best_ref[...] = jnp.full(best_ref.shape, NEVER, jnp.float32)

    def tile(turn, _):
        columns = pl.ds(pl.multiple_of(turn * size, size), size)

        def part(step, _):
            own_part = step < blocks // tall
            other_first = first + blocks - 2 * blocks * upper
            here = jnp.where(own_part, first + step * tall, other_first + step * tall - blocks)
            same = [
                [cluster_ref[here + i] == cluster_ref[first + turn * wide + j] for i in range(tall)]
                for j in range(wide)
            ]
            some = functools.reduce(jnp.logical_or, same[0] + same[1])

            @pl.when(some)
            def _():
                rows = pl.ds(pl.multiple_of(step * tall * BLOCK, tall * BLOCK), tall * BLOCK)
                product = products(chip_ref[rows, :], chip_ref[columns, :])
                row = lax.broadcasted_iota(jnp.int32, product.shape, 0) + step * tall * BLOCK
                column = lax.broadcasted_iota(jnp.int32, product.shape, 1) + turn * size
                product = jnp.where(row == column, NEVER, product)
                for j in range(wide):
                    at = pl.ds(turn * wide + j, 1)
                    best = best_ref[at, :]
                    for i in range(tall):
                        piece = product[i * BLOCK : (i + 1) * BLOCK, j * BLOCK : (j + 1) * BLOCK]
                        top = jnp.max(piece, axis=0, keepdims=True)
                        best = jnp.maximum(best, jnp.where(same[j][i], top, NEVER))
                    best_ref[at, :] = best

            return 0

        lax.fori_loop(0, 2 * blocks // tall, part, 0)
        return 0

    lax.fori_loop(0, blocks // wide, tile, 0)


def local_best(block_cluster, plan, rows, other):
    blocks = rows.shape[0] // BLOCK
    flops = 4 * rows.shape[0] * rows.shape[0] * rows.shape[1]
    vmem = pl.BlockSpec(memory_space=VMEM)
    return pl.pallas_call(
        local_kernel,
        out_shape=(
            VMEM((2 * rows.shape[0], rows.shape[1]), jnp.bfloat16),
            jax.ShapeDtypeStruct((blocks, BLOCK), jnp.float32),
        ),
        in_specs=[pl.BlockSpec(memory_space=SMEM)] * 2 + [vmem] * 2,
        out_specs=(vmem, vmem),
        compiler_params=pltpu.CompilerParams(vmem_limit_bytes=20 * MIB),
        cost_estimate=pl.CostEstimate(flops=flops, bytes_accessed=8 * rows.size, transcendentals=0),
    )(block_cluster, plan, rows, other)


def cross_kernel(start, tall, plan_ref, got_ref, chip_ref, *refs):
    blocks = chip_ref.shape[0] // BLOCK // 2
    wide = 2
    half = 16
    rows, row_best, chip_best = refs[-3:]
    back_ref, near_best_ref, far_best_ref = refs[-6:-3]
    count, near, far, upper = plan_ref[1], plan_ref[2], plan_ref[3], plan_ref[4]
    befores = refs[: len(refs) - 6]
    for ref, before in zip((near_best_ref, far_best_ref, back_ref), befores):
        ref[...] = before[...]
    for ref in (near_best_ref, far_best_ref, back_ref)[len(befores) :]:
        ref[...] = jnp.full(ref.shape, NEVER, jnp.float32)
    got_from = jnp.where(upper == 1, 0, blocks - count)
    got_to = got_from + count
    near_from = jnp.where(upper == 1, blocks - near, 0)
    far_from = blocks + jnp.where(upper == 1, blocks - far, 0)
    near_tile, far_tile = lax.div(near_from, wide), lax.div(far_from, wide)
    near_tiles = lax.div(near_from + near + wide - 1, wide) - near_tile
    far_tiles = lax.div(far_from + far + wide - 1, wide) - far_tile

    def part(step, _):
        at = pl.ds(pl.multiple_of(step * tall * BLOCK, tall * BLOCK), tall * BLOCK)
        rows[...] = unit(got_ref[at, :])
        row_best[...] = jnp.full(row_best.shape, NEVER, jnp.float32)
        first = start + step * tall
        fits_in = [(first + i >= got_from) & (first + i < got_to) for i in range(tall)]

        def tile(turn, _):
            turn = jnp.where(turn < near_tiles, near_tile + turn, far_tile + turn - near_tiles)
            side = chip_ref[pl.ds(pl.multiple_of(turn * wide * BLOCK, wide * BLOCK), wide * BLOCK), :]
            product = products(rows[...], side)
            for j in range(wide):
                block = turn * wide + j
                fits = ((block >= near_from) & (block < near_from + near)) | (
                    (block >= far_from) & (block < far_from + far)
                )
                best = jnp.full((1, BLOCK), NEVER, jnp.float32)
                for i in range(tall):
                    at = slice(i * BLOCK, (i + 1) * BLOCK)
                    piece = product[at, j * BLOCK : (j + 1) * BLOCK]
                    row_best[at, :] = jnp.maximum(row_best[at, :], jnp.where(fits, piece, NEVER))
                    top = jnp.max(piece, axis=0, keepdims=True)
                    best = jnp.maximum(best, jnp.where(fits_in[i] & fits, top, NEVER))
                at = pl.ds(jnp.where(block < blocks, block, block - blocks + half), 1)
                chip_best[at, :] = jnp.maximum(chip_best[at, :], best)
            return 0

        lax.fori_loop(0, near_tiles + far_tiles, tile, 0)
        for i in range(tall):
            top = jnp.max(row_best[i * BLOCK : (i + 1) * BLOCK, :].T, axis=0, keepdims=True)
            back_ref[pl.ds(first + i, 1), :] = jnp.where(fits_in[i], top, NEVER)
        return 0

    @pl.when(count > 0)
    def _():
        chip_best[...] = jnp.full(chip_best.shape, NEVER, jnp.float32)
        lax.fori_loop(0, got_ref.shape[0] // BLOCK // tall, part, 0)
        near_best_ref[...] = jnp.maximum(near_best_ref[...], chip_best[0:blocks, :])
        far_best_ref[...] = jnp.maximum(far_best_ref[...], chip_best[half : half + blocks, :])


def cross_best(plan, start, got, chip, before):
    blocks = chip.shape[0] // BLOCK // 2
    features = chip.shape[1]
    pieces = got.shape[0] // BLOCK
    tall = max(tall for tall in (1, 2, 3, 4) if pieces % tall == 0)
    out = jax.ShapeDtypeStruct((blocks, BLOCK), jnp.float32)
    vmem = pl.BlockSpec(memory_space=VMEM)
    flops = 2 * got.shape[0] * blocks * BLOCK * features
    return pl.pallas_call(
        functools.partial(cross_kernel, start, tall),
        out_shape=(out, out, out),
        in_specs=[pl.BlockSpec(memory_space=SMEM)] + [vmem] * (2 + len(before)),
        out_specs=(vmem, vmem, vmem),
        scratch_shapes=[
            VMEM((tall * BLOCK, features), jnp.bfloat16),
            VMEM((tall * BLOCK, BLOCK), jnp.float32),
            VMEM((32, BLOCK), jnp.float32),
        ],
        compiler_params=pltpu.CompilerParams(vmem_limit_bytes=16 * MIB),
        cost_estimate=pl.CostEstimate(flops=flops, bytes_accessed=4 * got.size, transcendentals=0),
    )(plan, got, chip, *before)


def on_device(embeddings, block_cluster, pair_blocks):
    blocks = embeddings.shape[0] // BLOCK
    devices = lax.axis_size("rows")
    swap = [(i, i ^ 1) for i in range(devices)]
    leftwards = [(i + 1, i) for i in range(1, devices - 1, 2)]
    rightwards = [(b, a) for a, b in leftwards]

    early = lax.ppermute(embeddings[: EARLY * BLOCK], "rows", leftwards)
    other = lax.ppermute(embeddings, "rows", swap)
    way, turn, plan = make_plan(block_cluster, 2 * blocks)

    def send(route, pieces):
        to_left = route is leftwards

        def branch(embeddings, other, early):
            starts = []
            done = EARLY if to_left else 0
            for piece in pieces:
                starts.append(done if to_left else blocks - done - piece)
                done += piece
            got = [
                lax.ppermute(embeddings[start * BLOCK : (start + piece) * BLOCK], "rows", route)
                for start, piece in zip(starts, pieces)
            ]
            chip, best = local_best(block_cluster, plan, embeddings, other)
            found = (best,)
            if to_left:
                starts, got = [0] + starts, [early] + got
            for start, piece in zip(starts, got):
                back, near, far = cross_best(plan, start, piece, chip, found)
                found = near, far, back
            return found

        return branch

    def stay(embeddings, other, early):
        _, best = local_best(block_cluster, plan, embeddings, other)
        nothing = jnp.full((blocks, BLOCK), NEVER, jnp.float32)
        return best, nothing, nothing

    sends = [send(leftwards, pieces) for pieces in LEFT_PIECES]
    sends += [send(rightwards, pieces) for pieces in RIGHT_PIECES]
    best, far_best, back = lax.switch(way[0], [stay] + sends, embeddings, other, early)

    from_core = lax.ppermute(far_best, "rows", swap)
    returned = lax.switch(
        turn[0],
        [
            lambda back: back,
            lambda back: lax.ppermute(back, "rows", rightwards),
            lambda back: lax.ppermute(back, "rows", leftwards),
        ],
        back,
    )
    best = jnp.maximum(best, from_core)
    best = jnp.where(plan[0] > 0, jnp.maximum(best, returned), best)
    return best.reshape(-1)


def solution(mesh):
    placed = (P(("groups", "rows"), None), P("groups"), P(("groups", "rows"), None))
    return jax.shard_map(
        on_device, mesh=mesh, in_specs=placed, out_specs=P(("groups", "rows")), check_vma=False
    )
```

```python
import functools

import jax
import jax.numpy as jnp
from jax import lax
from jax.experimental import pallas as pl
from jax.experimental.pallas import tpu as pltpu
from jax.sharding import PartitionSpec as P

BLOCK = 128
NEVER = -3.0
MIB = 1 << 20
FAR_AWAY = 1 << 20
SIZES = (4, 8, 11, 12)
PIECES = ((4,), (6, 2), (6, 3, 2), (6, 4, 2))
LEADING = 6
SMEM = pltpu.SMEM
VMEM = pltpu.VMEM


def plan_kernel(chip_blocks, cluster_ref, way_ref, plan_ref, left_part, right_part, from_left, turn):
    here = chip_blocks // 2
    chips = cluster_ref.shape[0] // chip_blocks
    me = lax.axis_index("rows")

    def run_length(start, step):
        count = jnp.int32(0)
        for jump in (16, 8, 4, 2, 1):
            further = count + jump
            same = cluster_ref[start + step * further] == cluster_ref[start]
            count = jnp.where(same, further, count)
        return count

    def cost(blocks):
        held = jnp.int32(0)
        for size, below in zip(SIZES, (0,) + SIZES):
            held = jnp.where(blocks > below, size, held)
        return jnp.where(blocks > here, FAR_AWAY, held)

    def forward(boundary, carry):
        best_left, best_right, load_right = carry
        edge = (boundary + 1) * chip_blocks
        behind = run_length(edge, -1)
        ahead = run_length(edge - 1, 1)
        left_part[boundary] = behind
        right_part[boundary] = ahead
        load_left = cost(ahead)
        by_left = jnp.maximum(best_left, load_left)
        by_right = jnp.maximum(best_right, load_right + load_left)
        from_left[boundary] = jnp.where(by_left <= by_right, 0, 1)
        stays_right = jnp.maximum(best_right, load_right)
        from_left[chips + boundary] = jnp.where(best_left <= stays_right, 0, 1)
        return jnp.minimum(by_left, by_right), jnp.minimum(best_left, stays_right), cost(behind)

    best_left, best_right, load_right = lax.fori_loop(
        0, chips - 1, forward, (jnp.int32(0), jnp.int32(FAR_AWAY), jnp.int32(0))
    )
    last = jnp.where(best_left <= jnp.maximum(best_right, load_right), 0, 1)

    def backward(step, state):
        boundary = chips - 2 - step
        turn[boundary] = state
        return from_left[state * chips + boundary]

    lax.fori_loop(0, chips - 1, backward, last)
    upper = lax.rem(me, 2)
    mine = lax.div(me, 2) - 1 + upper
    inside = (mine >= 0) & (mine < chips - 1)
    mine = jnp.clip(mine, 0, chips - 2)
    behind, ahead, rightwards = left_part[mine], right_part[mine], turn[mine]
    live = inside & (behind > 0) & (ahead > 0)
    receives = live & (rightwards != upper)
    sent = jnp.where(rightwards == 1, behind, ahead)
    paired = jnp.where(rightwards == 1, ahead, behind)
    middle = lax.div(me, 2) * chip_blocks + here
    below = jnp.minimum(run_length(middle, -1), here)
    above = jnp.minimum(run_length(middle - 1, 1), here)
    size = 1 + rightwards * len(SIZES)
    for bound in SIZES[:-1]:
        size = size + (sent > bound).astype(jnp.int32)
    way_ref[0] = jnp.where(live, size, 0)
    plan_ref[0] = (live & (rightwards == upper)).astype(jnp.int32)
    plan_ref[1] = jnp.where(receives, sent, 0)
    plan_ref[2] = jnp.where(receives, jnp.minimum(paired, here), 0)
    plan_ref[3] = jnp.where(receives, jnp.maximum(paired - here, 0), 0)
    plan_ref[4] = upper
    plan_ref[5] = me * here
    plan_ref[6] = jnp.where(upper == 1, above, below)
    plan_ref[7] = jnp.where(upper == 1, below, above)


def make_plan(block_cluster, chip_blocks):
    chips = block_cluster.shape[0] // chip_blocks
    return pl.pallas_call(
        functools.partial(plan_kernel, chip_blocks),
        out_shape=tuple(jax.ShapeDtypeStruct((n,), jnp.int32) for n in (1, 8)),
        in_specs=[pl.BlockSpec(memory_space=SMEM)],
        out_specs=(pl.BlockSpec(memory_space=SMEM),) * 2,
        scratch_shapes=[
            SMEM((chips,), jnp.int32),
            SMEM((chips,), jnp.int32),
            SMEM((2 * chips,), jnp.int32),
            SMEM((chips,), jnp.int32),
        ],
    )(block_cluster)


def unit(rows):
    broadened = rows.astype(jnp.float32)
    total = jnp.sum(broadened * broadened, axis=1, keepdims=True)
    return (broadened * lax.rsqrt(total + 1e-06)).astype(jnp.bfloat16)


def products(left, right):
    return lax.dot_general(
        left, right, (((1,), (1,)), ((), ())), preferred_element_type=jnp.float32
    )


def local_kernel(cluster_ref, plan_ref, rows_ref, other_ref, chip_ref, best_ref):
    blocks = rows_ref.shape[0] // BLOCK
    upper, first, theirs = plan_ref[4], plan_ref[5], plan_ref[7]
    tall, wide = 4, 2
    size = wide * BLOCK

    def normalise(turn, _):
        at = pl.ds(pl.multiple_of(turn * size, size), size)
        chip_ref[at, :] = unit(rows_ref[at, :])
        return 0

    lax.fori_loop(0, blocks // wide, normalise, 0)

    def normalise_other(turn, _):
        start = pl.multiple_of(turn * size, size)
        chip_ref[pl.ds(start + blocks * BLOCK, size), :] = unit(other_ref[pl.ds(start, size), :])
        return 0

    their_from = jnp.where(upper == 1, blocks - theirs, 0)
    their_tiles = lax.div(their_from, wide), lax.div(their_from + theirs + wide - 1, wide)
    lax.fori_loop(their_tiles[0], their_tiles[1], normalise_other, 0)
    best_ref[...] = jnp.full(best_ref.shape, NEVER, jnp.float32)

    def tile(turn, _):
        columns = pl.ds(pl.multiple_of(turn * size, size), size)

        def part(step, _):
            own_part = step < blocks // tall
            other_first = first + blocks - 2 * blocks * upper
            here = jnp.where(own_part, first + step * tall, other_first + step * tall - blocks)
            same = [
                [cluster_ref[here + i] == cluster_ref[first + turn * wide + j] for i in range(tall)]
                for j in range(wide)
            ]
            some = functools.reduce(jnp.logical_or, same[0] + same[1])

            @pl.when(some)
            def _():
                rows = pl.ds(pl.multiple_of(step * tall * BLOCK, tall * BLOCK), tall * BLOCK)
                product = products(chip_ref[rows, :], chip_ref[columns, :])
                row = lax.broadcasted_iota(jnp.int32, product.shape, 0) + step * tall * BLOCK
                column = lax.broadcasted_iota(jnp.int32, product.shape, 1) + turn * size
                product = jnp.where(row == column, NEVER, product)
                for j in range(wide):
                    at = pl.ds(turn * wide + j, 1)
                    best = best_ref[at, :]
                    for i in range(tall):
                        piece = product[i * BLOCK : (i + 1) * BLOCK, j * BLOCK : (j + 1) * BLOCK]
                        top = jnp.max(piece, axis=0, keepdims=True)
                        best = jnp.maximum(best, jnp.where(same[j][i], top, NEVER))
                    best_ref[at, :] = best

            return 0

        lax.fori_loop(0, 2 * blocks // tall, part, 0)
        return 0

    lax.fori_loop(0, blocks // wide, tile, 0)


def local_best(block_cluster, plan, rows, other):
    blocks = rows.shape[0] // BLOCK
    flops = 4 * rows.shape[0] * rows.shape[0] * rows.shape[1]
    vmem = pl.BlockSpec(memory_space=VMEM)
    return pl.pallas_call(
        local_kernel,
        out_shape=(
            VMEM((2 * rows.shape[0], rows.shape[1]), jnp.bfloat16),
            jax.ShapeDtypeStruct((blocks, BLOCK), jnp.float32),
        ),
        in_specs=[pl.BlockSpec(memory_space=SMEM)] * 2 + [vmem] * 2,
        out_specs=(vmem, vmem),
        compiler_params=pltpu.CompilerParams(vmem_limit_bytes=20 * MIB),
        cost_estimate=pl.CostEstimate(flops=flops, bytes_accessed=8 * rows.size, transcendentals=0),
    )(block_cluster, plan, rows, other)


def cross_kernel(start, tall, wide, plan_ref, got_ref, chip_ref, *refs):
    blocks = chip_ref.shape[0] // BLOCK // 2
    half = 16
    rows, row_best, chip_best = refs[-3:]
    back_ref, near_best_ref, far_best_ref = refs[-6:-3]
    count, near, far, upper = plan_ref[1], plan_ref[2], plan_ref[3], plan_ref[4]
    befores = refs[: len(refs) - 6]
    for ref, before in zip((near_best_ref, far_best_ref, back_ref), befores):
        ref[...] = before[...]
    for ref in (near_best_ref, far_best_ref, back_ref)[len(befores) :]:
        ref[...] = jnp.full(ref.shape, NEVER, jnp.float32)
    got_from = jnp.where(upper == 1, 0, blocks - count)
    got_to = got_from + count
    near_from = jnp.where(upper == 1, blocks - near, 0)
    far_from = blocks + jnp.where(upper == 1, blocks - far, 0)
    near_tile, far_tile = lax.div(near_from, wide), lax.div(far_from, wide)
    near_tiles = lax.div(near_from + near + wide - 1, wide) - near_tile
    far_tiles = lax.div(far_from + far + wide - 1, wide) - far_tile

    def part(step, _):
        at = pl.ds(pl.multiple_of(step * tall * BLOCK, tall * BLOCK), tall * BLOCK)
        rows[...] = unit(got_ref[at, :])
        row_best[...] = jnp.full(row_best.shape, NEVER, jnp.float32)
        first = start + step * tall
        fits_in = [(first + i >= got_from) & (first + i < got_to) for i in range(tall)]

        def tile(turn, _):
            turn = jnp.where(turn < near_tiles, near_tile + turn, far_tile + turn - near_tiles)
            side = chip_ref[pl.ds(pl.multiple_of(turn * wide * BLOCK, wide * BLOCK), wide * BLOCK), :]
            product = products(rows[...], side)
            for j in range(wide):
                block = turn * wide + j
                fits = ((block >= near_from) & (block < near_from + near)) | (
                    (block >= far_from) & (block < far_from + far)
                )
                best = jnp.full((1, BLOCK), NEVER, jnp.float32)
                for i in range(tall):
                    at = slice(i * BLOCK, (i + 1) * BLOCK)
                    piece = product[at, j * BLOCK : (j + 1) * BLOCK]
                    row_best[at, :] = jnp.maximum(row_best[at, :], jnp.where(fits, piece, NEVER))
                    top = jnp.max(piece, axis=0, keepdims=True)
                    best = jnp.maximum(best, jnp.where(fits_in[i] & fits, top, NEVER))
                at = pl.ds(jnp.where(block < blocks, block, block - blocks + half), 1)
                chip_best[at, :] = jnp.maximum(chip_best[at, :], best)
            return 0

        lax.fori_loop(0, near_tiles + far_tiles, tile, 0)
        for i in range(tall):
            top = jnp.max(row_best[i * BLOCK : (i + 1) * BLOCK, :].T, axis=0, keepdims=True)
            back_ref[pl.ds(first + i, 1), :] = jnp.where(fits_in[i], top, NEVER)
        return 0

    @pl.when(count > 0)
    def _():
        chip_best[...] = jnp.full(chip_best.shape, NEVER, jnp.float32)
        lax.fori_loop(0, got_ref.shape[0] // BLOCK // tall, part, 0)
        near_best_ref[...] = jnp.maximum(near_best_ref[...], chip_best[0:blocks, :])
        far_best_ref[...] = jnp.maximum(far_best_ref[...], chip_best[half : half + blocks, :])


def cross_best(plan, start, got, chip, before, wide):
    blocks = chip.shape[0] // BLOCK // 2
    features = chip.shape[1]
    pieces = got.shape[0] // BLOCK
    tall = max(tall for tall in (1, 2, 3, 4) if pieces % tall == 0)
    out = jax.ShapeDtypeStruct((blocks, BLOCK), jnp.float32)
    vmem = pl.BlockSpec(memory_space=VMEM)
    flops = 2 * got.shape[0] * blocks * BLOCK * features
    return pl.pallas_call(
        functools.partial(cross_kernel, start, tall, wide),
        out_shape=(out, out, out),
        in_specs=[pl.BlockSpec(memory_space=SMEM)] + [vmem] * (2 + len(before)),
        out_specs=(vmem, vmem, vmem),
        scratch_shapes=[
            VMEM((tall * BLOCK, features), jnp.bfloat16),
            VMEM((tall * BLOCK, BLOCK), jnp.float32),
            VMEM((32, BLOCK), jnp.float32),
        ],
        compiler_params=pltpu.CompilerParams(vmem_limit_bytes=16 * MIB),
        cost_estimate=pl.CostEstimate(flops=flops, bytes_accessed=4 * got.size, transcendentals=0),
    )(plan, got, chip, *before)


def on_device(embeddings, block_cluster, pair_blocks):
    blocks = embeddings.shape[0] // BLOCK
    devices = lax.axis_size("rows")
    swap = [(i, i ^ 1) for i in range(devices)]
    leftwards = [(i + 1, i) for i in range(1, devices - 1, 2)]
    rightwards = [(b, a) for a, b in leftwards]

    other = lax.ppermute(embeddings, "rows", swap)
    way, plan = make_plan(block_cluster, 2 * blocks)
    first, last = embeddings[: LEADING * BLOCK], embeddings[-LEADING * BLOCK :]

    def send(route, back_route, pieces):
        to_left = route is leftwards

        def branch(embeddings, first, last, other):
            starts = []
            done = 0
            for piece in pieces:
                starts.append(done if to_left else blocks - done - piece)
                done += piece
            got = []
            for start, piece in zip(starts, pieces):
                if piece == LEADING:
                    part = first if to_left else last
                else:
                    part = embeddings[start * BLOCK : (start + piece) * BLOCK]
                got.append(lax.ppermute(part, "rows", route))
            chip, best = local_best(block_cluster, plan, embeddings, other)
            found = (best,)
            for start, piece in zip(starts, got):
                wide = 4 if start == starts[-1] else 2
                back, near, far = cross_best(plan, start, piece, chip, found, wide)
                found = near, far, back
            return near, far, lax.ppermute(back, "rows", back_route)

        return branch

    def stay(embeddings, first, last, other):
        _, best = local_best(block_cluster, plan, embeddings, other)
        nothing = jnp.full((blocks, BLOCK), NEVER, jnp.float32)
        return best, nothing, nothing

    sends = [send(leftwards, rightwards, pieces) for pieces in PIECES]
    sends += [send(rightwards, leftwards, pieces) for pieces in PIECES]
    best, far_best, returned = lax.switch(
        way[0], [stay] + sends, embeddings, first, last, other
    )
    best = jnp.maximum(best, lax.ppermute(far_best, "rows", swap))
    best = jnp.where(plan[0] > 0, jnp.maximum(best, returned), best)
    return best.reshape(-1)


def solution(mesh):
    placed = (P(("groups", "rows"), None), P("groups"), P(("groups", "rows"), None))
    return jax.shard_map(
        on_device, mesh=mesh, in_specs=placed, out_specs=P(("groups", "rows")), check_vma=False
    )
```

```python
import functools

import jax
import jax.numpy as jnp
from jax import lax
from jax.experimental import pallas as pl
from jax.experimental.pallas import tpu as pltpu
from jax.sharding import PartitionSpec as P

BLOCK = 128
NEVER = -3.0
MIB = 1 << 20
FAR_AWAY = 1 << 20
SIZES = (4, 8, 11, 12)
PIECES = ((4,), (6, 2), (6, 3, 2), (6, 4, 2))
LEADING = 6
SMEM = pltpu.SMEM
VMEM = pltpu.VMEM


def plan_kernel(
    chip_blocks, cluster_ref, rows_ref, way_ref, plan_ref, first_ref, last_ref,
    left_part, right_part, from_left, turn, copied,
):
    size = first_ref.shape[0]
    copies = [
        pltpu.make_async_copy(rows_ref.at[pl.ds(start, size), :], ref, copied.at[index])
        for index, (start, ref) in enumerate(((0, first_ref), (rows_ref.shape[0] - size, last_ref)))
    ]
    for copy in copies:
        copy.start()
    here = chip_blocks // 2
    chips = cluster_ref.shape[0] // chip_blocks
    me = lax.axis_index("rows")

    def run_length(start, step):
        count = jnp.int32(0)
        for jump in (16, 8, 4, 2, 1):
            further = count + jump
            same = cluster_ref[start + step * further] == cluster_ref[start]
            count = jnp.where(same, further, count)
        return count

    def cost(blocks):
        held = jnp.int32(0)
        for size, below in zip(SIZES, (0,) + SIZES):
            held = jnp.where(blocks > below, size, held)
        return jnp.where(blocks > here, FAR_AWAY, held)

    def forward(boundary, carry):
        best_left, best_right, load_right = carry
        edge = (boundary + 1) * chip_blocks
        behind = run_length(edge, -1)
        ahead = run_length(edge - 1, 1)
        left_part[boundary] = behind
        right_part[boundary] = ahead
        load_left = cost(ahead)
        by_left = jnp.maximum(best_left, load_left)
        by_right = jnp.maximum(best_right, load_right + load_left)
        from_left[boundary] = jnp.where(by_left <= by_right, 0, 1)
        stays_right = jnp.maximum(best_right, load_right)
        from_left[chips + boundary] = jnp.where(best_left <= stays_right, 0, 1)
        return jnp.minimum(by_left, by_right), jnp.minimum(best_left, stays_right), cost(behind)

    best_left, best_right, load_right = lax.fori_loop(
        0, chips - 1, forward, (jnp.int32(0), jnp.int32(FAR_AWAY), jnp.int32(0))
    )
    last = jnp.where(best_left <= jnp.maximum(best_right, load_right), 0, 1)

    def backward(step, state):
        boundary = chips - 2 - step
        turn[boundary] = state
        return from_left[state * chips + boundary]

    lax.fori_loop(0, chips - 1, backward, last)
    upper = lax.rem(me, 2)
    mine = lax.div(me, 2) - 1 + upper
    inside = (mine >= 0) & (mine < chips - 1)
    mine = jnp.clip(mine, 0, chips - 2)
    behind, ahead, rightwards = left_part[mine], right_part[mine], turn[mine]
    live = inside & (behind > 0) & (ahead > 0)
    receives = live & (rightwards != upper)
    sent = jnp.where(rightwards == 1, behind, ahead)
    paired = jnp.where(rightwards == 1, ahead, behind)
    middle = lax.div(me, 2) * chip_blocks + here
    below = jnp.minimum(run_length(middle, -1), here)
    above = jnp.minimum(run_length(middle - 1, 1), here)
    branch = 1 + rightwards * len(SIZES)
    for bound in SIZES[:-1]:
        branch = branch + (sent > bound).astype(jnp.int32)
    way_ref[0] = jnp.where(live, branch, 0)
    plan_ref[0] = (live & (rightwards == upper)).astype(jnp.int32)
    plan_ref[1] = jnp.where(receives, sent, 0)
    plan_ref[2] = jnp.where(receives, jnp.minimum(paired, here), 0)
    plan_ref[3] = jnp.where(receives, jnp.maximum(paired - here, 0), 0)
    plan_ref[4] = upper
    plan_ref[5] = me * here
    plan_ref[6] = jnp.where(upper == 1, above, below)
    plan_ref[7] = jnp.where(upper == 1, below, above)
    for copy in copies:
        copy.wait()


def make_plan(block_cluster, rows, chip_blocks):
    chips = block_cluster.shape[0] // chip_blocks
    return pl.pallas_call(
        functools.partial(plan_kernel, chip_blocks),
        out_shape=tuple(jax.ShapeDtypeStruct((n,), jnp.int32) for n in (1, 8))
        + (VMEM((LEADING * BLOCK, rows.shape[1]), rows.dtype),) * 2,
        in_specs=[pl.BlockSpec(memory_space=SMEM), pl.BlockSpec(memory_space=pl.ANY)],
        out_specs=(pl.BlockSpec(memory_space=SMEM),) * 2 + (pl.BlockSpec(memory_space=VMEM),) * 2,
        scratch_shapes=[
            SMEM((chips,), jnp.int32),
            SMEM((chips,), jnp.int32),
            SMEM((2 * chips,), jnp.int32),
            SMEM((chips,), jnp.int32),
            pltpu.SemaphoreType.DMA((2,)),
        ],
    )(block_cluster, rows)


def unit(rows):
    broadened = rows.astype(jnp.float32)
    total = jnp.sum(broadened * broadened, axis=1, keepdims=True)
    return (broadened * lax.rsqrt(total + 1e-06)).astype(jnp.bfloat16)


def products(left, right):
    return lax.dot_general(
        left, right, (((1,), (1,)), ((), ())), preferred_element_type=jnp.float32
    )


def local_kernel(cluster_ref, plan_ref, rows_ref, other_ref, chip_ref, best_ref):
    blocks = rows_ref.shape[0] // BLOCK
    upper, first, theirs = plan_ref[4], plan_ref[5], plan_ref[7]
    tall, wide = 4, 2
    size = wide * BLOCK

    def normalise(turn, _):
        at = pl.ds(pl.multiple_of(turn * size, size), size)
        chip_ref[at, :] = unit(rows_ref[at, :])
        return 0

    lax.fori_loop(0, blocks // wide, normalise, 0)

    def normalise_other(turn, _):
        start = pl.multiple_of(turn * size, size)
        chip_ref[pl.ds(start + blocks * BLOCK, size), :] = unit(other_ref[pl.ds(start, size), :])
        return 0

    their_from = jnp.where(upper == 1, blocks - theirs, 0)
    their_tiles = lax.div(their_from, wide), lax.div(their_from + theirs + wide - 1, wide)
    lax.fori_loop(their_tiles[0], their_tiles[1], normalise_other, 0)
    best_ref[...] = jnp.full(best_ref.shape, NEVER, jnp.float32)

    def tile(turn, _):
        columns = pl.ds(pl.multiple_of(turn * size, size), size)

        def part(step, _):
            own_part = step < blocks // tall
            other_first = first + blocks - 2 * blocks * upper
            here = jnp.where(own_part, first + step * tall, other_first + step * tall - blocks)
            same = [
                [cluster_ref[here + i] == cluster_ref[first + turn * wide + j] for i in range(tall)]
                for j in range(wide)
            ]
            some = functools.reduce(jnp.logical_or, same[0] + same[1])

            @pl.when(some)
            def _():
                rows = pl.ds(pl.multiple_of(step * tall * BLOCK, tall * BLOCK), tall * BLOCK)
                product = products(chip_ref[rows, :], chip_ref[columns, :])
                row = lax.broadcasted_iota(jnp.int32, product.shape, 0) + step * tall * BLOCK
                column = lax.broadcasted_iota(jnp.int32, product.shape, 1) + turn * size
                product = jnp.where(row == column, NEVER, product)
                for j in range(wide):
                    at = pl.ds(turn * wide + j, 1)
                    best = best_ref[at, :]
                    for i in range(tall):
                        piece = product[i * BLOCK : (i + 1) * BLOCK, j * BLOCK : (j + 1) * BLOCK]
                        top = jnp.max(piece, axis=0, keepdims=True)
                        best = jnp.maximum(best, jnp.where(same[j][i], top, NEVER))
                    best_ref[at, :] = best

            return 0

        lax.fori_loop(0, 2 * blocks // tall, part, 0)
        return 0

    lax.fori_loop(0, blocks // wide, tile, 0)


def local_best(block_cluster, plan, rows, other):
    blocks = rows.shape[0] // BLOCK
    flops = 4 * rows.shape[0] * rows.shape[0] * rows.shape[1]
    vmem = pl.BlockSpec(memory_space=VMEM)
    return pl.pallas_call(
        local_kernel,
        out_shape=(
            VMEM((2 * rows.shape[0], rows.shape[1]), jnp.bfloat16),
            jax.ShapeDtypeStruct((blocks, BLOCK), jnp.float32),
        ),
        in_specs=[pl.BlockSpec(memory_space=SMEM)] * 2 + [vmem] * 2,
        out_specs=(vmem, vmem),
        compiler_params=pltpu.CompilerParams(vmem_limit_bytes=20 * MIB),
        cost_estimate=pl.CostEstimate(flops=flops, bytes_accessed=8 * rows.size, transcendentals=0),
    )(block_cluster, plan, rows, other)


def cross_kernel(start, tall, wide, plan_ref, got_ref, chip_ref, *refs):
    blocks = chip_ref.shape[0] // BLOCK // 2
    half = 16
    rows, row_best, chip_best = refs[-3:]
    back_ref, near_best_ref, far_best_ref = refs[-6:-3]
    count, near, far, upper = plan_ref[1], plan_ref[2], plan_ref[3], plan_ref[4]
    befores = refs[: len(refs) - 6]
    for ref, before in zip((near_best_ref, far_best_ref, back_ref), befores):
        ref[...] = before[...]
    for ref in (near_best_ref, far_best_ref, back_ref)[len(befores) :]:
        ref[...] = jnp.full(ref.shape, NEVER, jnp.float32)
    got_from = jnp.where(upper == 1, 0, blocks - count)
    got_to = got_from + count
    near_from = jnp.where(upper == 1, blocks - near, 0)
    far_from = blocks + jnp.where(upper == 1, blocks - far, 0)
    near_tile, far_tile = lax.div(near_from, wide), lax.div(far_from, wide)
    near_tiles = lax.div(near_from + near + wide - 1, wide) - near_tile
    far_tiles = lax.div(far_from + far + wide - 1, wide) - far_tile

    def part(step, _):
        at = pl.ds(pl.multiple_of(step * tall * BLOCK, tall * BLOCK), tall * BLOCK)
        rows[...] = unit(got_ref[at, :])
        row_best[...] = jnp.full(row_best.shape, NEVER, jnp.float32)
        first = start + step * tall
        fits_in = [(first + i >= got_from) & (first + i < got_to) for i in range(tall)]

        def tile(turn, _):
            turn = jnp.where(turn < near_tiles, near_tile + turn, far_tile + turn - near_tiles)
            side = chip_ref[pl.ds(pl.multiple_of(turn * wide * BLOCK, wide * BLOCK), wide * BLOCK), :]
            product = products(rows[...], side)
            for j in range(wide):
                block = turn * wide + j
                fits = ((block >= near_from) & (block < near_from + near)) | (
                    (block >= far_from) & (block < far_from + far)
                )
                best = jnp.full((1, BLOCK), NEVER, jnp.float32)
                for i in range(tall):
                    at = slice(i * BLOCK, (i + 1) * BLOCK)
                    piece = product[at, j * BLOCK : (j + 1) * BLOCK]
                    row_best[at, :] = jnp.maximum(row_best[at, :], jnp.where(fits, piece, NEVER))
                    top = jnp.max(piece, axis=0, keepdims=True)
                    best = jnp.maximum(best, jnp.where(fits_in[i] & fits, top, NEVER))
                at = pl.ds(jnp.where(block < blocks, block, block - blocks + half), 1)
                chip_best[at, :] = jnp.maximum(chip_best[at, :], best)
            return 0

        lax.fori_loop(0, near_tiles + far_tiles, tile, 0)
        for i in range(tall):
            top = jnp.max(row_best[i * BLOCK : (i + 1) * BLOCK, :].T, axis=0, keepdims=True)
            back_ref[pl.ds(first + i, 1), :] = jnp.where(fits_in[i], top, NEVER)
        return 0

    @pl.when(count > 0)
    def _():
        chip_best[...] = jnp.full(chip_best.shape, NEVER, jnp.float32)
        lax.fori_loop(0, got_ref.shape[0] // BLOCK // tall, part, 0)
        near_best_ref[...] = jnp.maximum(near_best_ref[...], chip_best[0:blocks, :])
        far_best_ref[...] = jnp.maximum(far_best_ref[...], chip_best[half : half + blocks, :])


def cross_best(plan, start, got, chip, before, wide):
    blocks = chip.shape[0] // BLOCK // 2
    features = chip.shape[1]
    pieces = got.shape[0] // BLOCK
    tall = max(tall for tall in (1, 2, 3, 4) if pieces % tall == 0)
    out = jax.ShapeDtypeStruct((blocks, BLOCK), jnp.float32)
    vmem = pl.BlockSpec(memory_space=VMEM)
    flops = 2 * got.shape[0] * blocks * BLOCK * features
    return pl.pallas_call(
        functools.partial(cross_kernel, start, tall, wide),
        out_shape=(out, out, out),
        in_specs=[pl.BlockSpec(memory_space=SMEM)] + [vmem] * (2 + len(before)),
        out_specs=(vmem, vmem, vmem),
        scratch_shapes=[
            VMEM((tall * BLOCK, features), jnp.bfloat16),
            VMEM((tall * BLOCK, BLOCK), jnp.float32),
            VMEM((32, BLOCK), jnp.float32),
        ],
        compiler_params=pltpu.CompilerParams(vmem_limit_bytes=16 * MIB),
        cost_estimate=pl.CostEstimate(flops=flops, bytes_accessed=4 * got.size, transcendentals=0),
    )(plan, got, chip, *before)


def on_device(embeddings, block_cluster, pair_blocks):
    blocks = embeddings.shape[0] // BLOCK
    devices = lax.axis_size("rows")
    swap = [(i, i ^ 1) for i in range(devices)]
    leftwards = [(i + 1, i) for i in range(1, devices - 1, 2)]
    rightwards = [(b, a) for a, b in leftwards]

    other = lax.ppermute(embeddings, "rows", swap)
    way, plan, first, last = make_plan(block_cluster, embeddings, 2 * blocks)

    def send(route, back_route, pieces):
        to_left = route is leftwards

        def branch(embeddings, first, last, other):
            starts = []
            done = 0
            for piece in pieces:
                starts.append(done if to_left else blocks - done - piece)
                done += piece
            got = []
            for start, piece in zip(starts, pieces):
                if piece == LEADING:
                    part = first if to_left else last
                else:
                    part = embeddings[start * BLOCK : (start + piece) * BLOCK]
                got.append(lax.ppermute(part, "rows", route))
            chip, best = local_best(block_cluster, plan, embeddings, other)
            found = (best,)
            for start, piece in zip(starts, got):
                wide = 4 if start == starts[-1] else 2
                back, near, far = cross_best(plan, start, piece, chip, found, wide)
                found = near, far, back
            return near, far, lax.ppermute(back, "rows", back_route)

        return branch

    def stay(embeddings, first, last, other):
        _, best = local_best(block_cluster, plan, embeddings, other)
        nothing = jnp.full((blocks, BLOCK), NEVER, jnp.float32)
        return best, nothing, nothing

    sends = [send(leftwards, rightwards, pieces) for pieces in PIECES]
    sends += [send(rightwards, leftwards, pieces) for pieces in PIECES]
    best, far_best, returned = lax.switch(
        way[0], [stay] + sends, embeddings, first, last, other
    )
    best = jnp.maximum(best, lax.ppermute(far_best, "rows", swap))
    best = jnp.where(plan[0] > 0, jnp.maximum(best, returned), best)
    return best.reshape(-1)


def solution(mesh):
    placed = (P(("groups", "rows"), None), P("groups"), P(("groups", "rows"), None))
    return jax.shard_map(
        on_device, mesh=mesh, in_specs=placed, out_specs=P(("groups", "rows")), check_vma=False
    )
```

```python
import functools

import jax
import jax.numpy as jnp
from jax import lax
from jax.experimental import pallas as pl
from jax.experimental.pallas import tpu as pltpu
from jax.sharding import PartitionSpec as P

BLOCK = 128
NEVER = -3.0
MIB = 1 << 20
FAR_AWAY = 1 << 20
SIZES = (4, 8, 11, 12)
PIECES = ((4,), (6, 2), (6, 3, 2), (6, 4, 2))
LEADING = 6
SMEM = pltpu.SMEM
VMEM = pltpu.VMEM


def plan_kernel(
    chip_blocks, cluster_ref, rows_ref, way_ref, plan_ref, first_ref, last_ref,
    left_part, right_part, from_left, turn, copied,
):
    size = first_ref.shape[0]
    copies = [
        pltpu.make_async_copy(rows_ref.at[pl.ds(start, size), :], ref, copied.at[index])
        for index, (start, ref) in enumerate(((0, first_ref), (rows_ref.shape[0] - size, last_ref)))
    ]
    for copy in copies:
        copy.start()
    here = chip_blocks // 2
    chips = cluster_ref.shape[0] // chip_blocks
    me = lax.axis_index("rows")

    def run_length(start, step, limit):
        count = jnp.int32(0)
        for jump in (16, 8, 4, 2, 1):
            if jump <= limit:
                further = count + jump
                at = jnp.clip(start + step * further, 0, cluster_ref.shape[0] - 1)
                same = (cluster_ref[at] == cluster_ref[start]) & (further <= limit)
                count = jnp.where(same, further, count)
        return count

    def cost(blocks):
        held = jnp.int32(0)
        for size, below in zip(SIZES, (0,) + SIZES):
            held = jnp.where(blocks > below, size, held)
        return jnp.where(blocks > here, FAR_AWAY, held)

    def forward(boundary, carry):
        best_left, best_right, load_right = carry
        edge = (boundary + 1) * chip_blocks
        behind = run_length(edge, -1, chip_blocks - 1)
        ahead = run_length(edge - 1, 1, chip_blocks - 1)
        left_part[boundary] = behind
        right_part[boundary] = ahead
        load_left = cost(ahead)
        by_left = jnp.maximum(best_left, load_left)
        by_right = jnp.maximum(best_right, load_right + load_left)
        from_left[boundary] = jnp.where(by_left <= by_right, 0, 1)
        stays_right = jnp.maximum(best_right, load_right)
        from_left[chips + boundary] = jnp.where(best_left <= stays_right, 0, 1)
        return jnp.minimum(by_left, by_right), jnp.minimum(best_left, stays_right), cost(behind)

    best_left, best_right, load_right = lax.fori_loop(
        0, chips - 1, forward, (jnp.int32(0), jnp.int32(FAR_AWAY), jnp.int32(0))
    )
    last = jnp.where(best_left <= jnp.maximum(best_right, load_right), 0, 1)

    def backward(step, state):
        boundary = chips - 2 - step
        turn[boundary] = state
        return from_left[state * chips + boundary]

    lax.fori_loop(0, chips - 1, backward, last)
    upper = lax.rem(me, 2)
    mine = lax.div(me, 2) - 1 + upper
    inside = (mine >= 0) & (mine < chips - 1)
    mine = jnp.clip(mine, 0, chips - 2)
    behind, ahead, rightwards = left_part[mine], right_part[mine], turn[mine]
    live = inside & (behind > 0) & (ahead > 0)
    receives = live & (rightwards != upper)
    sent = jnp.where(rightwards == 1, behind, ahead)
    paired = jnp.where(rightwards == 1, ahead, behind)
    middle = lax.div(me, 2) * chip_blocks + here
    below = run_length(middle, -1, here)
    above = run_length(middle - 1, 1, here)
    branch = 1 + rightwards * len(SIZES)
    for bound in SIZES[:-1]:
        branch = branch + (sent > bound).astype(jnp.int32)
    way_ref[0] = jnp.where(live, branch, 0)
    plan_ref[0] = (live & (rightwards == upper)).astype(jnp.int32)
    plan_ref[1] = jnp.where(receives, sent, 0)
    plan_ref[2] = jnp.where(receives, jnp.minimum(paired, here), 0)
    plan_ref[3] = jnp.where(receives, jnp.maximum(paired - here, 0), 0)
    plan_ref[4] = upper
    plan_ref[5] = me * here
    plan_ref[6] = jnp.where(upper == 1, above, below)
    plan_ref[7] = jnp.where(upper == 1, below, above)
    for copy in copies:
        copy.wait()


def make_plan(block_cluster, rows, chip_blocks):
    chips = block_cluster.shape[0] // chip_blocks
    return pl.pallas_call(
        functools.partial(plan_kernel, chip_blocks),
        out_shape=tuple(jax.ShapeDtypeStruct((n,), jnp.int32) for n in (1, 8))
        + (VMEM((LEADING * BLOCK, rows.shape[1]), rows.dtype),) * 2,
        in_specs=[pl.BlockSpec(memory_space=SMEM), pl.BlockSpec(memory_space=pl.ANY)],
        out_specs=(pl.BlockSpec(memory_space=SMEM),) * 2 + (pl.BlockSpec(memory_space=VMEM),) * 2,
        scratch_shapes=[
            SMEM((chips,), jnp.int32),
            SMEM((chips,), jnp.int32),
            SMEM((2 * chips,), jnp.int32),
            SMEM((chips,), jnp.int32),
            pltpu.SemaphoreType.DMA((2,)),
        ],
    )(block_cluster, rows)


def unit(rows):
    broadened = rows.astype(jnp.float32)
    total = jnp.sum(broadened * broadened, axis=1, keepdims=True)
    return (broadened * lax.rsqrt(total + 1e-06)).astype(jnp.bfloat16)


def products(left, right):
    return lax.dot_general(
        left, right, (((1,), (1,)), ((), ())), preferred_element_type=jnp.float32
    )


def local_kernel(cluster_ref, plan_ref, rows_ref, other_ref, chip_ref, best_ref):
    blocks = rows_ref.shape[0] // BLOCK
    upper, first, theirs = plan_ref[4], plan_ref[5], plan_ref[7]
    tall, wide = 4, 2
    size = wide * BLOCK

    def normalise(turn, _):
        at = pl.ds(pl.multiple_of(turn * size, size), size)
        chip_ref[at, :] = unit(rows_ref[at, :])
        return 0

    lax.fori_loop(0, blocks // wide, normalise, 0)

    def normalise_other(turn, _):
        start = pl.multiple_of(turn * size, size)
        chip_ref[pl.ds(start + blocks * BLOCK, size), :] = unit(other_ref[pl.ds(start, size), :])
        return 0

    their_from = jnp.where(upper == 1, blocks - theirs, 0)
    their_tiles = lax.div(their_from, wide), lax.div(their_from + theirs + wide - 1, wide)
    lax.fori_loop(their_tiles[0], their_tiles[1], normalise_other, 0)
    best_ref[...] = jnp.full(best_ref.shape, NEVER, jnp.float32)

    def tile(turn, _):
        columns = pl.ds(pl.multiple_of(turn * size, size), size)

        def part(step, _):
            own_part = step < blocks // tall
            other_first = first + blocks - 2 * blocks * upper
            here = jnp.where(own_part, first + step * tall, other_first + step * tall - blocks)
            same = [
                [cluster_ref[here + i] == cluster_ref[first + turn * wide + j] for i in range(tall)]
                for j in range(wide)
            ]
            some = functools.reduce(jnp.logical_or, same[0] + same[1])

            @pl.when(some)
            def _():
                rows = pl.ds(pl.multiple_of(step * tall * BLOCK, tall * BLOCK), tall * BLOCK)
                product = products(chip_ref[rows, :], chip_ref[columns, :])
                row = lax.broadcasted_iota(jnp.int32, product.shape, 0) + step * tall * BLOCK
                column = lax.broadcasted_iota(jnp.int32, product.shape, 1) + turn * size
                product = jnp.where(row == column, NEVER, product)
                for j in range(wide):
                    at = pl.ds(turn * wide + j, 1)
                    best = best_ref[at, :]
                    for i in range(tall):
                        piece = product[i * BLOCK : (i + 1) * BLOCK, j * BLOCK : (j + 1) * BLOCK]
                        top = jnp.max(piece, axis=0, keepdims=True)
                        best = jnp.maximum(best, jnp.where(same[j][i], top, NEVER))
                    best_ref[at, :] = best

            return 0

        lax.fori_loop(0, 2 * blocks // tall, part, 0)
        return 0

    lax.fori_loop(0, blocks // wide, tile, 0)


def local_best(block_cluster, plan, rows, other):
    blocks = rows.shape[0] // BLOCK
    flops = 4 * rows.shape[0] * rows.shape[0] * rows.shape[1]
    vmem = pl.BlockSpec(memory_space=VMEM)
    return pl.pallas_call(
        local_kernel,
        out_shape=(
            VMEM((2 * rows.shape[0], rows.shape[1]), jnp.bfloat16),
            jax.ShapeDtypeStruct((blocks, BLOCK), jnp.float32),
        ),
        in_specs=[pl.BlockSpec(memory_space=SMEM)] * 2 + [vmem] * 2,
        out_specs=(vmem, vmem),
        compiler_params=pltpu.CompilerParams(vmem_limit_bytes=20 * MIB),
        cost_estimate=pl.CostEstimate(flops=flops, bytes_accessed=8 * rows.size, transcendentals=0),
    )(block_cluster, plan, rows, other)


def cross_kernel(start, tall, wide, plan_ref, got_ref, chip_ref, *refs):
    blocks = chip_ref.shape[0] // BLOCK // 2
    half = 16
    rows, row_best, chip_best = refs[-3:]
    back_ref, near_best_ref, far_best_ref = refs[-6:-3]
    count, near, far, upper = plan_ref[1], plan_ref[2], plan_ref[3], plan_ref[4]
    befores = refs[: len(refs) - 6]
    for ref, before in zip((near_best_ref, far_best_ref, back_ref), befores):
        ref[...] = before[...]
    for ref in (near_best_ref, far_best_ref, back_ref)[len(befores) :]:
        ref[...] = jnp.full(ref.shape, NEVER, jnp.float32)
    got_from = jnp.where(upper == 1, 0, blocks - count)
    got_to = got_from + count
    near_from = jnp.where(upper == 1, blocks - near, 0)
    far_from = blocks + jnp.where(upper == 1, blocks - far, 0)
    near_tile, far_tile = lax.div(near_from, wide), lax.div(far_from, wide)
    near_tiles = lax.div(near_from + near + wide - 1, wide) - near_tile
    far_tiles = lax.div(far_from + far + wide - 1, wide) - far_tile

    def part(step, _):
        at = pl.ds(pl.multiple_of(step * tall * BLOCK, tall * BLOCK), tall * BLOCK)
        rows[...] = unit(got_ref[at, :])
        row_best[...] = jnp.full(row_best.shape, NEVER, jnp.float32)
        first = start + step * tall
        fits_in = [(first + i >= got_from) & (first + i < got_to) for i in range(tall)]

        def tile(turn, _):
            turn = jnp.where(turn < near_tiles, near_tile + turn, far_tile + turn - near_tiles)
            side = chip_ref[pl.ds(pl.multiple_of(turn * wide * BLOCK, wide * BLOCK), wide * BLOCK), :]
            product = products(rows[...], side)
            for j in range(wide):
                block = turn * wide + j
                fits = ((block >= near_from) & (block < near_from + near)) | (
                    (block >= far_from) & (block < far_from + far)
                )
                best = jnp.full((1, BLOCK), NEVER, jnp.float32)
                for i in range(tall):
                    at = slice(i * BLOCK, (i + 1) * BLOCK)
                    piece = product[at, j * BLOCK : (j + 1) * BLOCK]
                    row_best[at, :] = jnp.maximum(row_best[at, :], jnp.where(fits, piece, NEVER))
                    top = jnp.max(piece, axis=0, keepdims=True)
                    best = jnp.maximum(best, jnp.where(fits_in[i] & fits, top, NEVER))
                at = pl.ds(jnp.where(block < blocks, block, block - blocks + half), 1)
                chip_best[at, :] = jnp.maximum(chip_best[at, :], best)
            return 0

        lax.fori_loop(0, near_tiles + far_tiles, tile, 0)
        for i in range(tall):
            top = jnp.max(row_best[i * BLOCK : (i + 1) * BLOCK, :].T, axis=0, keepdims=True)
            back_ref[pl.ds(first + i, 1), :] = jnp.where(fits_in[i], top, NEVER)
        return 0

    @pl.when(count > 0)
    def _():
        chip_best[...] = jnp.full(chip_best.shape, NEVER, jnp.float32)
        lax.fori_loop(0, got_ref.shape[0] // BLOCK // tall, part, 0)
        near_best_ref[...] = jnp.maximum(near_best_ref[...], chip_best[0:blocks, :])
        far_best_ref[...] = jnp.maximum(far_best_ref[...], chip_best[half : half + blocks, :])


def cross_best(plan, start, got, chip, before, wide):
    blocks = chip.shape[0] // BLOCK // 2
    features = chip.shape[1]
    pieces = got.shape[0] // BLOCK
    tall = max(tall for tall in (1, 2, 3, 4) if pieces % tall == 0)
    out = jax.ShapeDtypeStruct((blocks, BLOCK), jnp.float32)
    vmem = pl.BlockSpec(memory_space=VMEM)
    flops = 2 * got.shape[0] * blocks * BLOCK * features
    return pl.pallas_call(
        functools.partial(cross_kernel, start, tall, wide),
        out_shape=(out, out, out),
        in_specs=[pl.BlockSpec(memory_space=SMEM)] + [vmem] * (2 + len(before)),
        out_specs=(vmem, vmem, vmem),
        scratch_shapes=[
            VMEM((tall * BLOCK, features), jnp.bfloat16),
            VMEM((tall * BLOCK, BLOCK), jnp.float32),
            VMEM((32, BLOCK), jnp.float32),
        ],
        compiler_params=pltpu.CompilerParams(vmem_limit_bytes=16 * MIB),
        cost_estimate=pl.CostEstimate(flops=flops, bytes_accessed=4 * got.size, transcendentals=0),
    )(plan, got, chip, *before)


def on_device(embeddings, block_cluster, pair_blocks):
    blocks = embeddings.shape[0] // BLOCK
    devices = lax.axis_size("rows")
    swap = [(i, i ^ 1) for i in range(devices)]
    leftwards = [(i + 1, i) for i in range(1, devices - 1, 2)]
    rightwards = [(b, a) for a, b in leftwards]

    other = lax.ppermute(embeddings, "rows", swap)
    way, plan, first, last = make_plan(block_cluster, embeddings, 2 * blocks)

    def send(route, back_route, pieces):
        to_left = route is leftwards

        def branch(embeddings, first, last, other):
            starts = []
            done = 0
            for piece in pieces:
                starts.append(done if to_left else blocks - done - piece)
                done += piece
            got = []
            for start, piece in zip(starts, pieces):
                if piece == LEADING:
                    part = first if to_left else last
                else:
                    part = embeddings[start * BLOCK : (start + piece) * BLOCK]
                got.append(lax.ppermute(part, "rows", route))
            chip, best = local_best(block_cluster, plan, embeddings, other)
            found = (best,)
            for start, piece in zip(starts, got):
                wide = 4 if start == starts[-1] else 2
                back, near, far = cross_best(plan, start, piece, chip, found, wide)
                found = near, far, back
            return near, far, lax.ppermute(back, "rows", back_route)

        return branch

    def stay(embeddings, first, last, other):
        _, best = local_best(block_cluster, plan, embeddings, other)
        nothing = jnp.full((blocks, BLOCK), NEVER, jnp.float32)
        return best, nothing, nothing

    sends = [send(leftwards, rightwards, pieces) for pieces in PIECES]
    sends += [send(rightwards, leftwards, pieces) for pieces in PIECES]
    best, far_best, returned = lax.switch(
        way[0], [stay] + sends, embeddings, first, last, other
    )
    best = jnp.maximum(best, lax.ppermute(far_best, "rows", swap))
    best = jnp.where(plan[0] > 0, jnp.maximum(best, returned), best)
    return best.reshape(-1)


def solution(mesh):
    placed = (P(("groups", "rows"), None), P("groups"), P(("groups", "rows"), None))
    return jax.shard_map(
        on_device, mesh=mesh, in_specs=placed, out_specs=P(("groups", "rows")), check_vma=False
    )
```

```python
import functools

import jax
import jax.numpy as jnp
from jax import lax
from jax.experimental import pallas as pl
from jax.experimental.pallas import tpu as pltpu
from jax.sharding import PartitionSpec as P

BLOCK = 128
NEVER = -3.0
MIB = 1 << 20
FAR_AWAY = 1 << 20
SIZES = (4, 8, 11, 12)
PIECES = ((4,), (6, 2), (6, 3, 2), (6, 4, 2))
LEADING = 6
SMEM = pltpu.SMEM
VMEM = pltpu.VMEM


def plan_kernel(
    chip_blocks, cluster_ref, rows_ref, way_ref, plan_ref, first_ref, last_ref,
    left_part, right_part, from_left, turn, copied,
):
    size = first_ref.shape[0]
    copies = [
        pltpu.make_async_copy(rows_ref.at[pl.ds(start, size), :], ref, copied.at[index])
        for index, (start, ref) in enumerate(((0, first_ref), (rows_ref.shape[0] - size, last_ref)))
    ]
    for copy in copies:
        copy.start()
    here = chip_blocks // 2
    chips = cluster_ref.shape[0] // chip_blocks
    me = lax.axis_index("rows")

    def run_length(start, step, limit):
        count = jnp.int32(0)
        for jump in (16, 8, 4, 2, 1):
            if jump <= limit:
                further = count + jump
                at = jnp.clip(start + step * further, 0, cluster_ref.shape[0] - 1)
                same = (cluster_ref[at] == cluster_ref[start]) & (further <= limit)
                count = jnp.where(same, further, count)
        return count

    def cost(blocks):
        held = jnp.int32(0)
        for size, below in zip(SIZES, (0,) + SIZES):
            held = jnp.where(blocks > below, size, held)
        return jnp.where(blocks > here, FAR_AWAY, held)

    def forward(boundary, carry):
        best_left, best_right, load_right = carry
        edge = (boundary + 1) * chip_blocks
        behind = run_length(edge, -1, chip_blocks - 1)
        ahead = run_length(edge - 1, 1, chip_blocks - 1)
        left_part[boundary] = behind
        right_part[boundary] = ahead
        load_left = cost(ahead)
        by_left = jnp.maximum(best_left, load_left)
        by_right = jnp.maximum(best_right, load_right + load_left)
        from_left[boundary] = jnp.where(by_left <= by_right, 0, 1)
        stays_right = jnp.maximum(best_right, load_right)
        from_left[chips + boundary] = jnp.where(best_left <= stays_right, 0, 1)
        return jnp.minimum(by_left, by_right), jnp.minimum(best_left, stays_right), cost(behind)

    best_left, best_right, load_right = lax.fori_loop(
        0, chips - 1, forward, (jnp.int32(0), jnp.int32(FAR_AWAY), jnp.int32(0))
    )
    last = jnp.where(best_left <= jnp.maximum(best_right, load_right), 0, 1)

    def backward(step, state):
        boundary = chips - 2 - step
        turn[boundary] = state
        return from_left[state * chips + boundary]

    lax.fori_loop(0, chips - 1, backward, last)
    upper = lax.rem(me, 2)
    mine = lax.div(me, 2) - 1 + upper
    inside = (mine >= 0) & (mine < chips - 1)
    mine = jnp.clip(mine, 0, chips - 2)
    behind, ahead, rightwards = left_part[mine], right_part[mine], turn[mine]
    live = inside & (behind > 0) & (ahead > 0)
    receives = live & (rightwards != upper)
    sent = jnp.where(rightwards == 1, behind, ahead)
    paired = jnp.where(rightwards == 1, ahead, behind)
    middle = lax.div(me, 2) * chip_blocks + here
    below = run_length(middle, -1, here)
    above = run_length(middle - 1, 1, here)
    branch = 1 + rightwards * len(SIZES)
    for bound in SIZES[:-1]:
        branch = branch + (sent > bound).astype(jnp.int32)
    way_ref[0] = jnp.where(live, branch, 0)
    plan_ref[0] = jnp.where(receives, sent, 0)
    plan_ref[1] = jnp.where(receives, jnp.minimum(paired, here), 0)
    plan_ref[2] = jnp.where(receives, jnp.maximum(paired - here, 0), 0)
    plan_ref[3] = upper
    plan_ref[4] = me * here
    plan_ref[5] = jnp.where(upper == 1, above, below)
    plan_ref[6] = jnp.where(upper == 1, below, above)
    for copy in copies:
        copy.wait()


def make_plan(block_cluster, rows, chip_blocks):
    chips = block_cluster.shape[0] // chip_blocks
    return pl.pallas_call(
        functools.partial(plan_kernel, chip_blocks),
        out_shape=tuple(jax.ShapeDtypeStruct((n,), jnp.int32) for n in (1, 7))
        + (VMEM((LEADING * BLOCK, rows.shape[1]), rows.dtype),) * 2,
        in_specs=[pl.BlockSpec(memory_space=SMEM), pl.BlockSpec(memory_space=pl.ANY)],
        out_specs=(pl.BlockSpec(memory_space=SMEM),) * 2 + (pl.BlockSpec(memory_space=VMEM),) * 2,
        scratch_shapes=[
            SMEM((chips,), jnp.int32),
            SMEM((chips,), jnp.int32),
            SMEM((2 * chips,), jnp.int32),
            SMEM((chips,), jnp.int32),
            pltpu.SemaphoreType.DMA((2,)),
        ],
    )(block_cluster, rows)


def unit(rows):
    broadened = rows.astype(jnp.float32)
    total = jnp.sum(broadened * broadened, axis=1, keepdims=True)
    return (broadened * lax.rsqrt(total + 1e-06)).astype(jnp.bfloat16)


def products(left, right):
    return lax.dot_general(
        left, right, (((1,), (1,)), ((), ())), preferred_element_type=jnp.float32
    )


def local_kernel(cluster_ref, plan_ref, rows_ref, other_ref, chip_ref, best_ref):
    blocks = rows_ref.shape[0] // BLOCK
    upper, first, theirs = plan_ref[3], plan_ref[4], plan_ref[6]
    tall, wide = 4, 2
    size = wide * BLOCK

    def normalise(turn, _):
        at = pl.ds(pl.multiple_of(turn * size, size), size)
        chip_ref[at, :] = unit(rows_ref[at, :])
        return 0

    lax.fori_loop(0, blocks // wide, normalise, 0)

    def normalise_other(turn, _):
        start = pl.multiple_of(turn * size, size)
        chip_ref[pl.ds(start + blocks * BLOCK, size), :] = unit(other_ref[pl.ds(start, size), :])
        return 0

    their_from = jnp.where(upper == 1, blocks - theirs, 0)
    their_tiles = lax.div(their_from, wide), lax.div(their_from + theirs + wide - 1, wide)
    lax.fori_loop(their_tiles[0], their_tiles[1], normalise_other, 0)
    best_ref[...] = jnp.full(best_ref.shape, NEVER, jnp.float32)

    def tile(turn, _):
        columns = pl.ds(pl.multiple_of(turn * size, size), size)

        def part(step, _):
            own_part = step < blocks // tall
            other_first = first + blocks - 2 * blocks * upper
            here = jnp.where(own_part, first + step * tall, other_first + step * tall - blocks)
            same = [
                [cluster_ref[here + i] == cluster_ref[first + turn * wide + j] for i in range(tall)]
                for j in range(wide)
            ]
            some = functools.reduce(jnp.logical_or, same[0] + same[1])

            @pl.when(some)
            def _():
                rows = pl.ds(pl.multiple_of(step * tall * BLOCK, tall * BLOCK), tall * BLOCK)
                product = products(chip_ref[rows, :], chip_ref[columns, :])
                row = lax.broadcasted_iota(jnp.int32, product.shape, 0) + step * tall * BLOCK
                column = lax.broadcasted_iota(jnp.int32, product.shape, 1) + turn * size
                product = jnp.where(row == column, NEVER, product)
                for j in range(wide):
                    at = pl.ds(turn * wide + j, 1)
                    best = best_ref[at, :]
                    for i in range(tall):
                        piece = product[i * BLOCK : (i + 1) * BLOCK, j * BLOCK : (j + 1) * BLOCK]
                        top = jnp.max(piece, axis=0, keepdims=True)
                        best = jnp.maximum(best, jnp.where(same[j][i], top, NEVER))
                    best_ref[at, :] = best

            return 0

        lax.fori_loop(0, 2 * blocks // tall, part, 0)
        return 0

    lax.fori_loop(0, blocks // wide, tile, 0)


def local_best(block_cluster, plan, rows, other):
    blocks = rows.shape[0] // BLOCK
    flops = 4 * rows.shape[0] * rows.shape[0] * rows.shape[1]
    vmem = pl.BlockSpec(memory_space=VMEM)
    return pl.pallas_call(
        local_kernel,
        out_shape=(
            VMEM((2 * rows.shape[0], rows.shape[1]), jnp.bfloat16),
            jax.ShapeDtypeStruct((blocks, BLOCK), jnp.float32),
        ),
        in_specs=[pl.BlockSpec(memory_space=SMEM)] * 2 + [vmem] * 2,
        out_specs=(vmem, vmem),
        compiler_params=pltpu.CompilerParams(vmem_limit_bytes=20 * MIB),
        cost_estimate=pl.CostEstimate(flops=flops, bytes_accessed=8 * rows.size, transcendentals=0),
    )(block_cluster, plan, rows, other)


def cross_kernel(start, tall, wide, plan_ref, got_ref, chip_ref, *refs):
    blocks = chip_ref.shape[0] // BLOCK // 2
    half = 16
    rows, row_best, chip_best = refs[-3:]
    back_ref, near_best_ref, far_best_ref = refs[-6:-3]
    whole = tall == 2
    count, near, far, upper = plan_ref[0], plan_ref[1], plan_ref[2], plan_ref[3]
    befores = refs[: len(refs) - 6]
    for ref, before in zip((near_best_ref, far_best_ref, back_ref), befores):
        ref[...] = before[...]
    for ref in (near_best_ref, far_best_ref, back_ref)[len(befores) :]:
        ref[...] = jnp.full(ref.shape, NEVER, jnp.float32)
    got_from = jnp.where(upper == 1, 0, blocks - count)
    got_to = got_from + count
    near_from = jnp.where(upper == 1, blocks - near, 0)
    far_from = blocks + jnp.where(upper == 1, blocks - far, 0)
    near_tile, far_tile = lax.div(near_from, wide), lax.div(far_from, wide)
    near_tiles = lax.div(near_from + near + wide - 1, wide) - near_tile
    far_tiles = lax.div(far_from + far + wide - 1, wide) - far_tile

    def part(step, _):
        at = pl.ds(pl.multiple_of(step * tall * BLOCK, tall * BLOCK), tall * BLOCK)
        rows[...] = unit(got_ref[at, :])
        row_best[...] = jnp.full(row_best.shape, NEVER, jnp.float32)
        first = start + step * tall
        fits_in = [(first + i >= got_from) & (first + i < got_to) for i in range(tall)]

        def tile(turn, _, lowest, wide):
            if whole and wide == blocks:
                side = chip_ref[: blocks * BLOCK, :]
            else:
                side = chip_ref[pl.ds(pl.multiple_of(lowest * BLOCK, wide * BLOCK), wide * BLOCK), :]
            product = products(rows[...], side)
            for j in range(wide):
                block = lowest + j
                fits = ((block >= near_from) & (block < near_from + near)) | (
                    (block >= far_from) & (block < far_from + far)
                )
                best = jnp.full((1, BLOCK), NEVER, jnp.float32)
                for i in range(tall):
                    at = slice(i * BLOCK, (i + 1) * BLOCK)
                    piece = product[at, j * BLOCK : (j + 1) * BLOCK]
                    row_best[at, :] = jnp.maximum(row_best[at, :], jnp.where(fits, piece, NEVER))
                    top = jnp.max(piece, axis=0, keepdims=True)
                    best = jnp.maximum(best, jnp.where(fits_in[i] & fits, top, NEVER))
                at = pl.ds(jnp.where(block < blocks, block, block - blocks + half), 1)
                chip_best[at, :] = jnp.maximum(chip_best[at, :], best)
            return 0

        def one_of_both(turn, _):
            turn = jnp.where(turn < near_tiles, near_tile + turn, far_tile + turn - near_tiles)
            return tile(turn, 0, turn * wide, wide)

        if whole:
            tile(0, 0, 0, blocks)
            lax.fori_loop(far_tile, far_tile + far_tiles, lambda turn, _: tile(turn, 0, turn * wide, wide), 0)
        else:
            lax.fori_loop(0, near_tiles + far_tiles, one_of_both, 0)
        for i in range(tall):
            top = jnp.max(row_best[i * BLOCK : (i + 1) * BLOCK, :].T, axis=0, keepdims=True)
            back_ref[pl.ds(first + i, 1), :] = jnp.where(fits_in[i], top, NEVER)
        return 0

    @pl.when(count > 0)
    def _():
        chip_best[...] = jnp.full(chip_best.shape, NEVER, jnp.float32)
        lax.fori_loop(0, got_ref.shape[0] // BLOCK // tall, part, 0)
        near_best_ref[...] = jnp.maximum(near_best_ref[...], chip_best[0:blocks, :])
        far_best_ref[...] = jnp.maximum(far_best_ref[...], chip_best[half : half + blocks, :])


def cross_best(plan, start, got, chip, before, wide):
    blocks = chip.shape[0] // BLOCK // 2
    features = chip.shape[1]
    pieces = got.shape[0] // BLOCK
    tall = max(tall for tall in (1, 2, 3, 4) if pieces % tall == 0)
    out = jax.ShapeDtypeStruct((blocks, BLOCK), jnp.float32)
    vmem = pl.BlockSpec(memory_space=VMEM)
    flops = 2 * got.shape[0] * blocks * BLOCK * features
    return pl.pallas_call(
        functools.partial(cross_kernel, start, tall, wide),
        out_shape=(out, out, out),
        in_specs=[pl.BlockSpec(memory_space=SMEM)] + [vmem] * (2 + len(before)),
        out_specs=(vmem, vmem, vmem),
        scratch_shapes=[
            VMEM((tall * BLOCK, features), jnp.bfloat16),
            VMEM((tall * BLOCK, BLOCK), jnp.float32),
            VMEM((32, BLOCK), jnp.float32),
        ],
        compiler_params=pltpu.CompilerParams(vmem_limit_bytes=16 * MIB),
        cost_estimate=pl.CostEstimate(flops=flops, bytes_accessed=4 * got.size, transcendentals=0),
    )(plan, got, chip, *before)


def on_device(embeddings, block_cluster, pair_blocks):
    blocks = embeddings.shape[0] // BLOCK
    devices = lax.axis_size("rows")
    swap = [(i, i ^ 1) for i in range(devices)]
    leftwards = [(i + 1, i) for i in range(1, devices - 1, 2)]
    rightwards = [(b, a) for a, b in leftwards]
    upper = lax.rem(lax.axis_index("rows"), 2)

    other = lax.ppermute(embeddings, "rows", swap)
    way, plan, first, last = make_plan(block_cluster, embeddings, 2 * blocks)

    def send(route, back_route, pieces):
        to_left = route is leftwards

        def branch(embeddings, first, last, other):
            starts = []
            done = 0
            for piece in pieces:
                starts.append(done if to_left else blocks - done - piece)
                done += piece
            got = []
            for start, piece in zip(starts, pieces):
                if piece == LEADING:
                    part = first if to_left else last
                else:
                    part = embeddings[start * BLOCK : (start + piece) * BLOCK]
                got.append(lax.ppermute(part, "rows", route))
            chip, best = local_best(block_cluster, plan, embeddings, other)
            found = (best,)
            for start, piece in zip(starts, got):
                wide = 2
                back, near, far = cross_best(plan, start, piece, chip, found, wide)
                found = near, far, back
            returned = lax.ppermute(back, "rows", back_route)
            sender = upper == (0 if to_left else 1)
            return jnp.maximum(near, jnp.where(sender, returned, NEVER)), far

        return branch

    def stay(embeddings, first, last, other):
        _, best = local_best(block_cluster, plan, embeddings, other)
        return best, jnp.full((blocks, BLOCK), NEVER, jnp.float32)

    sends = [send(leftwards, rightwards, pieces) for pieces in PIECES]
    sends += [send(rightwards, leftwards, pieces) for pieces in PIECES]
    best, far_best = lax.switch(way[0], [stay] + sends, embeddings, first, last, other)
    return jnp.maximum(best, lax.ppermute(far_best, "rows", swap)).reshape(-1)


def solution(mesh):
    placed = (P(("groups", "rows"), None), P("groups"), P(("groups", "rows"), None))
    return jax.shard_map(
        on_device, mesh=mesh, in_specs=placed, out_specs=P(("groups", "rows")), check_vma=False
    )
```

```python
import functools

import jax
import jax.numpy as jnp
from jax import lax
from jax.experimental import pallas as pl
from jax.experimental.pallas import tpu as pltpu
from jax.sharding import PartitionSpec as P

BLOCK = 128
NEVER = -3.0
MIB = 1 << 20
FAR_AWAY = 1 << 20
SIZES = (4, 11, 12, 14)
PIECES = ((4,), (6, 3, 2), (6, 4, 2), (6, 4, 2, 2))
LEADING = 6
BACK_ROWS = 16
STEP = 128
SMEM = pltpu.SMEM
VMEM = pltpu.VMEM


def plan_kernel(
    chip_blocks, cluster_ref, rows_ref, way_ref, plan_ref, first_ref, last_ref,
    left_part, right_part, from_left, turn, copied,
):
    size = first_ref.shape[0]
    copies = [
        pltpu.make_async_copy(rows_ref.at[pl.ds(start, size), :], ref, copied.at[index])
        for index, (start, ref) in enumerate(((0, first_ref), (rows_ref.shape[0] - size, last_ref)))
    ]
    for copy in copies:
        copy.start()
    here = chip_blocks // 2
    chips = cluster_ref.shape[0] // chip_blocks
    me = lax.axis_index("rows")

    def run_length(start, step, limit):
        count = jnp.int32(0)
        for jump in (16, 8, 4, 2, 1):
            if jump <= limit:
                further = count + jump
                at = jnp.clip(start + step * further, 0, cluster_ref.shape[0] - 1)
                same = (cluster_ref[at] == cluster_ref[start]) & (further <= limit)
                count = jnp.where(same, further, count)
        return count

    def cost(blocks):
        held = jnp.int32(0)
        for size, below in zip(SIZES, (0,) + SIZES):
            held = jnp.where(blocks > below, size, held)
        return jnp.where(blocks > SIZES[-1], FAR_AWAY, held)

    def forward(boundary, carry):
        best_left, best_right, load_right = carry
        edge = (boundary + 1) * chip_blocks
        behind = run_length(edge, -1, chip_blocks - 1)
        ahead = run_length(edge - 1, 1, chip_blocks - 1)
        left_part[boundary] = behind
        right_part[boundary] = ahead
        load_left = cost(ahead)
        by_left = jnp.maximum(best_left, load_left)
        by_right = jnp.maximum(best_right, load_right + load_left)
        from_left[boundary] = jnp.where(by_left <= by_right, 0, 1)
        stays_right = jnp.maximum(best_right, load_right)
        from_left[chips + boundary] = jnp.where(best_left <= stays_right, 0, 1)
        return jnp.minimum(by_left, by_right), jnp.minimum(best_left, stays_right), cost(behind)

    best_left, best_right, load_right = lax.fori_loop(
        0, chips - 1, forward, (jnp.int32(0), jnp.int32(FAR_AWAY), jnp.int32(0))
    )
    last = jnp.where(best_left <= jnp.maximum(best_right, load_right), 0, 1)

    def backward(step, state):
        boundary = chips - 2 - step
        turn[boundary] = state
        return from_left[state * chips + boundary]

    lax.fori_loop(0, chips - 1, backward, last)
    upper = lax.rem(me, 2)
    mine = lax.div(me, 2) - 1 + upper
    inside = (mine >= 0) & (mine < chips - 1)
    mine = jnp.clip(mine, 0, chips - 2)
    behind, ahead, rightwards = left_part[mine], right_part[mine], turn[mine]
    live = inside & (behind > 0) & (ahead > 0)
    receives = live & (rightwards != upper)
    sent = jnp.where(rightwards == 1, behind, ahead)
    paired = jnp.where(rightwards == 1, ahead, behind)
    middle = lax.div(me, 2) * chip_blocks + here
    below = run_length(middle, -1, here)
    above = run_length(middle - 1, 1, here)
    branch = 1 + rightwards * len(SIZES)
    for bound in SIZES[:-1]:
        branch = branch + (sent > bound).astype(jnp.int32)
    way_ref[0] = jnp.where(live, branch, 0)
    plan_ref[0] = jnp.where(receives, sent, 0)
    plan_ref[1] = jnp.where(receives, jnp.minimum(paired, here), 0)
    plan_ref[2] = jnp.where(receives, jnp.maximum(paired - here, 0), 0)
    plan_ref[3] = upper
    plan_ref[4] = me * here
    plan_ref[5] = jnp.where(upper == 1, above, below)
    plan_ref[6] = jnp.where(upper == 1, below, above)
    for copy in copies:
        copy.wait()


def make_plan(block_cluster, rows, chip_blocks):
    chips = block_cluster.shape[0] // chip_blocks
    return pl.pallas_call(
        functools.partial(plan_kernel, chip_blocks),
        out_shape=tuple(jax.ShapeDtypeStruct((n,), jnp.int32) for n in (1, 7))
        + (VMEM((LEADING * BLOCK, rows.shape[1]), rows.dtype),) * 2,
        in_specs=[pl.BlockSpec(memory_space=SMEM), pl.BlockSpec(memory_space=pl.ANY)],
        out_specs=(pl.BlockSpec(memory_space=SMEM),) * 2 + (pl.BlockSpec(memory_space=VMEM),) * 2,
        scratch_shapes=[
            SMEM((chips,), jnp.int32),
            SMEM((chips,), jnp.int32),
            SMEM((2 * chips,), jnp.int32),
            SMEM((chips,), jnp.int32),
            pltpu.SemaphoreType.DMA((2,)),
        ],
    )(block_cluster, rows)


def unit(rows):
    broadened = rows.astype(jnp.float32)
    total = jnp.sum(broadened * broadened, axis=1, keepdims=True)
    return (broadened * lax.rsqrt(total + 1e-06)).astype(jnp.bfloat16)


def unit_rows(source, target, start, to, count, step):
    def some(turn, _):
        at = pl.multiple_of(turn * step, step)
        target[pl.ds(to + at, step), :] = unit(source[pl.ds(start + at, step), :])
        return 0

    lax.fori_loop(0, count // step, some, 0)


def products(left, right):
    return lax.dot_general(
        left, right, (((1,), (1,)), ((), ())), preferred_element_type=jnp.float32
    )


def local_kernel(cluster_ref, plan_ref, rows_ref, other_ref, chip_ref, best_ref):
    blocks = rows_ref.shape[0] // BLOCK
    upper, first, theirs = plan_ref[3], plan_ref[4], plan_ref[6]
    tall, wide = 4, 2
    size = wide * BLOCK

    unit_rows(rows_ref, chip_ref, 0, 0, blocks * BLOCK, STEP)

    def normalise_other(turn, _):
        start = pl.multiple_of(turn * size, size)
        to = pl.multiple_of(start + blocks * BLOCK, size)
        unit_rows(other_ref, chip_ref, start, to, size, STEP)
        return 0

    their_from = jnp.where(upper == 1, blocks - theirs, 0)
    their_tiles = lax.div(their_from, wide), lax.div(their_from + theirs + wide - 1, wide)
    lax.fori_loop(their_tiles[0], their_tiles[1], normalise_other, 0)
    best_ref[...] = jnp.full(best_ref.shape, NEVER, jnp.float32)

    def tile(turn, _):
        columns = pl.ds(pl.multiple_of(turn * size, size), size)

        def part(step, _):
            own_part = step < blocks // tall
            other_first = first + blocks - 2 * blocks * upper
            here = jnp.where(own_part, first + step * tall, other_first + step * tall - blocks)
            same = [
                [cluster_ref[here + i] == cluster_ref[first + turn * wide + j] for i in range(tall)]
                for j in range(wide)
            ]
            some = functools.reduce(jnp.logical_or, same[0] + same[1])

            @pl.when(some)
            def _():
                rows = pl.ds(pl.multiple_of(step * tall * BLOCK, tall * BLOCK), tall * BLOCK)
                product = products(chip_ref[rows, :], chip_ref[columns, :])
                row = lax.broadcasted_iota(jnp.int32, product.shape, 0) + step * tall * BLOCK
                column = lax.broadcasted_iota(jnp.int32, product.shape, 1) + turn * size
                product = jnp.where(row == column, NEVER, product)
                for j in range(wide):
                    at = pl.ds(turn * wide + j, 1)
                    best = best_ref[at, :]
                    for i in range(tall):
                        piece = product[i * BLOCK : (i + 1) * BLOCK, j * BLOCK : (j + 1) * BLOCK]
                        top = jnp.max(piece, axis=0, keepdims=True)
                        best = jnp.maximum(best, jnp.where(same[j][i], top, NEVER))
                    best_ref[at, :] = best

            return 0

        lax.fori_loop(0, 2 * blocks // tall, part, 0)
        return 0

    lax.fori_loop(0, blocks // wide, tile, 0)


def local_best(block_cluster, plan, rows, other):
    blocks = rows.shape[0] // BLOCK
    flops = 4 * rows.shape[0] * rows.shape[0] * rows.shape[1]
    vmem = pl.BlockSpec(memory_space=VMEM)
    return pl.pallas_call(
        local_kernel,
        out_shape=(
            VMEM((2 * rows.shape[0], rows.shape[1]), jnp.bfloat16),
            jax.ShapeDtypeStruct((blocks, BLOCK), jnp.float32),
        ),
        in_specs=[pl.BlockSpec(memory_space=SMEM)] * 2 + [vmem] * 2,
        out_specs=(vmem, vmem),
        compiler_params=pltpu.CompilerParams(vmem_limit_bytes=20 * MIB),
        cost_estimate=pl.CostEstimate(flops=flops, bytes_accessed=8 * rows.size, transcendentals=0),
    )(block_cluster, plan, rows, other)


def cross_kernel(start, tall, wide, whole, plan_ref, got_ref, chip_ref, *refs):
    blocks = chip_ref.shape[0] // BLOCK // 2
    half = 16
    rows, row_best, chip_best = refs[-3:]
    back_ref, near_best_ref, far_best_ref = refs[-6:-3]
    count, near, far, upper = plan_ref[0], plan_ref[1], plan_ref[2], plan_ref[3]
    befores = refs[: len(refs) - 6]
    for ref, before in zip((near_best_ref, far_best_ref, back_ref), befores):
        ref[...] = before[...]
    for ref in (near_best_ref, far_best_ref, back_ref)[len(befores) :]:
        ref[...] = jnp.full(ref.shape, NEVER, jnp.float32)
    got_from = jnp.where(upper == 1, 0, blocks - count)
    got_to = got_from + count
    near_from = jnp.where(upper == 1, blocks - near, 0)
    far_from = blocks + jnp.where(upper == 1, blocks - far, 0)
    near_tile, far_tile = lax.div(near_from, wide), lax.div(far_from, wide)
    near_tiles = lax.div(near_from + near + wide - 1, wide) - near_tile
    far_tiles = lax.div(far_from + far + wide - 1, wide) - far_tile

    def part(step, _):
        first = start + step * tall
        fits_in = [(first + i >= got_from) & (first + i < got_to) for i in range(tall)]

        @pl.when(functools.reduce(jnp.logical_or, fits_in))
        def _():
            at = pl.multiple_of(step * tall * BLOCK, tall * BLOCK)
            unit_rows(got_ref, rows, at, 0, tall * BLOCK, tall * BLOCK if whole else STEP)
            row_best[...] = jnp.full(row_best.shape, NEVER, jnp.float32)

            def tile(turn, _, lowest, wide):
                if whole and wide == blocks:
                    side = chip_ref[: blocks * BLOCK, :]
                else:
                    side = chip_ref[pl.ds(pl.multiple_of(lowest * BLOCK, wide * BLOCK), wide * BLOCK), :]
                product = products(rows[...], side)
                for j in range(wide):
                    block = lowest + j
                    fits = ((block >= near_from) & (block < near_from + near)) | (
                        (block >= far_from) & (block < far_from + far)
                    )
                    best = jnp.full((1, BLOCK), NEVER, jnp.float32)
                    for i in range(tall):
                        at = slice(i * BLOCK, (i + 1) * BLOCK)
                        piece = product[at, j * BLOCK : (j + 1) * BLOCK]
                        row_best[at, :] = jnp.maximum(row_best[at, :], jnp.where(fits, piece, NEVER))
                        top = jnp.max(piece, axis=0, keepdims=True)
                        best = jnp.maximum(best, jnp.where(fits_in[i] & fits, top, NEVER))
                    at = pl.ds(jnp.where(block < blocks, block, block - blocks + half), 1)
                    chip_best[at, :] = jnp.maximum(chip_best[at, :], best)
                return 0

            def one_of_both(turn, _):
                turn = jnp.where(turn < near_tiles, near_tile + turn, far_tile + turn - near_tiles)
                return tile(turn, 0, turn * wide, wide)

            if whole:
                tile(0, 0, 0, blocks)
                lax.fori_loop(far_tile, far_tile + far_tiles, lambda turn, _: tile(turn, 0, turn * wide, wide), 0)
            else:
                lax.fori_loop(0, near_tiles + far_tiles, one_of_both, 0)
            for i in range(tall):
                top = jnp.max(row_best[i * BLOCK : (i + 1) * BLOCK, :].T, axis=0, keepdims=True)
                at = pl.ds(start % BACK_ROWS + step * tall + i, 1)
                back_ref[at, :] = jnp.where(fits_in[i], top, NEVER)

        return 0

    @pl.when(count > 0)
    def _():
        chip_best[...] = jnp.full(chip_best.shape, NEVER, jnp.float32)
        lax.fori_loop(0, got_ref.shape[0] // BLOCK // tall, part, 0)
        near_best_ref[...] = jnp.maximum(near_best_ref[...], chip_best[0:blocks, :])
        far_best_ref[...] = jnp.maximum(far_best_ref[...], chip_best[half : half + blocks, :])


def cross_best(plan, start, got, chip, before, whole):
    blocks = chip.shape[0] // BLOCK // 2
    features = chip.shape[1]
    pieces = got.shape[0] // BLOCK
    tall = max(tall for tall in (1, 2, 3, 4) if pieces % tall == 0)
    out = jax.ShapeDtypeStruct((blocks, BLOCK), jnp.float32)
    vmem = pl.BlockSpec(memory_space=VMEM)
    flops = 2 * got.shape[0] * blocks * BLOCK * features
    return pl.pallas_call(
        functools.partial(cross_kernel, start, tall, 2, whole),
        out_shape=(jax.ShapeDtypeStruct((BACK_ROWS, BLOCK), jnp.float32), out, out),
        in_specs=[pl.BlockSpec(memory_space=SMEM)] + [vmem] * (2 + len(before)),
        out_specs=(vmem, vmem, vmem),
        scratch_shapes=[
            VMEM((tall * BLOCK, features), jnp.bfloat16),
            VMEM((tall * BLOCK, BLOCK), jnp.float32),
            VMEM((32, BLOCK), jnp.float32),
        ],
        compiler_params=pltpu.CompilerParams(vmem_limit_bytes=16 * MIB),
        cost_estimate=pl.CostEstimate(flops=flops, bytes_accessed=4 * got.size, transcendentals=0),
    )(plan, got, chip, *before)


def on_device(embeddings, block_cluster, pair_blocks):
    blocks = embeddings.shape[0] // BLOCK
    devices = lax.axis_size("rows")
    swap = [(i, i ^ 1) for i in range(devices)]
    leftwards = [(i + 1, i) for i in range(1, devices - 1, 2)]
    rightwards = [(b, a) for a, b in leftwards]
    upper = lax.rem(lax.axis_index("rows"), 2)

    other = lax.ppermute(embeddings, "rows", swap)
    way, plan, first, last = make_plan(block_cluster, embeddings, 2 * blocks)

    def send(route, back_route, pieces):
        to_left = route is leftwards

        def branch(embeddings, first, last, other):
            starts = []
            done = 0
            for piece in pieces:
                starts.append(done if to_left else blocks - done - piece)
                done += piece
            got = []
            for start, piece in zip(starts, pieces):
                if piece == LEADING:
                    part = first if to_left else last
                elif 0 <= start < blocks:
                    part = embeddings[start * BLOCK : (start + piece) * BLOCK]
                else:
                    part = other[: piece * BLOCK] if to_left else other[-piece * BLOCK :]
                got.append(lax.ppermute(part, "rows", route))
            chip, best = local_best(block_cluster, plan, embeddings, other)
            found = (best,)
            for start, piece in zip(starts, got):
                back, near, far = cross_best(plan, start, piece, chip, found, piece.shape[0] == 2 * BLOCK and start == starts[-1])
                found = near, far, back
            returned = lax.ppermute(back, "rows", back_route)
            sender = upper == (0 if to_left else 1)
            beyond = sum(pieces) - blocks
            if beyond > 0:
                theirs = returned[blocks : blocks + beyond] if to_left else returned[-beyond:]
                nothing = jnp.full((blocks - beyond, BLOCK), NEVER, jnp.float32)
                theirs = jnp.concatenate([theirs, nothing] if to_left else [nothing, theirs], axis=0)
                far = jnp.where(sender, theirs, far)
            return jnp.maximum(near, jnp.where(sender, returned[:blocks], NEVER)), far

        return branch

    def stay(embeddings, first, last, other):
        _, best = local_best(block_cluster, plan, embeddings, other)
        return best, jnp.full((blocks, BLOCK), NEVER, jnp.float32)

    sends = [send(leftwards, rightwards, pieces) for pieces in PIECES]
    sends += [send(rightwards, leftwards, pieces) for pieces in PIECES]
    best, far_best = lax.switch(way[0], [stay] + sends, embeddings, first, last, other)
    return jnp.maximum(best, lax.ppermute(far_best, "rows", swap)).reshape(-1)


def solution(mesh):
    placed = (P(("groups", "rows"), None), P("groups"), P(("groups", "rows"), None))
    return jax.shard_map(
        on_device, mesh=mesh, in_specs=placed, out_specs=P(("groups", "rows")), check_vma=False
    )
```

```python
import functools

import jax
import jax.numpy as jnp
from jax import lax
from jax.experimental import pallas as pl
from jax.experimental.pallas import tpu as pltpu
from jax.sharding import PartitionSpec as P

BLOCK = 128
NEVER = -3.0
MIB = 1 << 20
FAR_AWAY = 1 << 20
SIZES = (4, 11, 12, 14)
PIECES = ((4,), (6, 3, 2), (6, 4, 2), (6, 4, 2, 2))
LEADING = 6
BACK_ROWS = 16
STEP = 128
SMEM = pltpu.SMEM
VMEM = pltpu.VMEM


def plan_kernel(
    chip_blocks, cluster_ref, rows_ref, way_ref, plan_ref, first_ref, last_ref,
    left_part, right_part, from_left, turn, copied,
):
    size = first_ref.shape[0]
    copies = [
        pltpu.make_async_copy(rows_ref.at[pl.ds(start, size), :], ref, copied.at[index])
        for index, (start, ref) in enumerate(((0, first_ref), (rows_ref.shape[0] - size, last_ref)))
    ]
    for copy in copies:
        copy.start()
    here = chip_blocks // 2
    chips = cluster_ref.shape[0] // chip_blocks
    me = lax.axis_index("rows")

    def run_length(start, step, limit):
        count = jnp.int32(0)
        for jump in (16, 8, 4, 2, 1):
            if jump <= limit:
                further = count + jump
                at = jnp.clip(start + step * further, 0, cluster_ref.shape[0] - 1)
                same = (cluster_ref[at] == cluster_ref[start]) & (further <= limit)
                count = jnp.where(same, further, count)
        return count

    def cost(blocks):
        held = jnp.int32(0)
        for size, below in zip(SIZES, (0,) + SIZES):
            held = jnp.where(blocks > below, size, held)
        return jnp.where(blocks > SIZES[-1], FAR_AWAY, held)

    def forward(boundary, carry):
        best_left, best_right, load_right = carry
        edge = (boundary + 1) * chip_blocks
        behind = run_length(edge, -1, chip_blocks - 1)
        ahead = run_length(edge - 1, 1, chip_blocks - 1)
        left_part[boundary] = behind
        right_part[boundary] = ahead
        load_left = cost(ahead)
        by_left = jnp.maximum(best_left, load_left)
        by_right = jnp.maximum(best_right, load_right + load_left)
        from_left[boundary] = jnp.where(by_left <= by_right, 0, 1)
        stays_right = jnp.maximum(best_right, load_right)
        from_left[chips + boundary] = jnp.where(best_left <= stays_right, 0, 1)
        return jnp.minimum(by_left, by_right), jnp.minimum(best_left, stays_right), cost(behind)

    best_left, best_right, load_right = lax.fori_loop(
        0, chips - 1, forward, (jnp.int32(0), jnp.int32(FAR_AWAY), jnp.int32(0))
    )
    last = jnp.where(best_left <= jnp.maximum(best_right, load_right), 0, 1)

    def backward(step, state):
        boundary = chips - 2 - step
        turn[boundary] = state
        return from_left[state * chips + boundary]

    lax.fori_loop(0, chips - 1, backward, last)
    upper = lax.rem(me, 2)
    mine = lax.div(me, 2) - 1 + upper
    inside = (mine >= 0) & (mine < chips - 1)
    mine = jnp.clip(mine, 0, chips - 2)
    behind, ahead, rightwards = left_part[mine], right_part[mine], turn[mine]
    live = inside & (behind > 0) & (ahead > 0)
    receives = live & (rightwards != upper)
    sent = jnp.where(rightwards == 1, behind, ahead)
    paired = jnp.where(rightwards == 1, ahead, behind)
    middle = lax.div(me, 2) * chip_blocks + here
    below = run_length(middle, -1, here)
    above = run_length(middle - 1, 1, here)
    branch = 1 + rightwards * len(SIZES)
    for bound in SIZES[:-1]:
        branch = branch + (sent > bound).astype(jnp.int32)
    way_ref[0] = jnp.where(live, branch, 0)
    plan_ref[0] = jnp.where(receives, sent, 0)
    plan_ref[1] = jnp.where(receives, jnp.minimum(paired, here), 0)
    plan_ref[2] = jnp.where(receives, jnp.maximum(paired - here, 0), 0)
    plan_ref[3] = upper
    plan_ref[4] = me * here
    plan_ref[5] = jnp.where(upper == 1, above, below)
    plan_ref[6] = jnp.where(upper == 1, below, above)
    for copy in copies:
        copy.wait()


def make_plan(block_cluster, rows, chip_blocks):
    chips = block_cluster.shape[0] // chip_blocks
    return pl.pallas_call(
        functools.partial(plan_kernel, chip_blocks),
        out_shape=tuple(jax.ShapeDtypeStruct((n,), jnp.int32) for n in (1, 7))
        + (VMEM((LEADING * BLOCK, rows.shape[1]), rows.dtype),) * 2,
        in_specs=[pl.BlockSpec(memory_space=SMEM), pl.BlockSpec(memory_space=pl.ANY)],
        out_specs=(pl.BlockSpec(memory_space=SMEM),) * 2 + (pl.BlockSpec(memory_space=VMEM),) * 2,
        scratch_shapes=[
            SMEM((chips,), jnp.int32),
            SMEM((chips,), jnp.int32),
            SMEM((2 * chips,), jnp.int32),
            SMEM((chips,), jnp.int32),
            pltpu.SemaphoreType.DMA((2,)),
        ],
    )(block_cluster, rows)


def unit(rows):
    broadened = rows.astype(jnp.float32)
    total = jnp.sum(broadened * broadened, axis=1, keepdims=True)
    return (broadened * lax.rsqrt(total + 1e-06)).astype(jnp.bfloat16)


def unit_rows(source, target, start, to, count, step):
    def some(turn, _):
        at = pl.multiple_of(turn * step, step)
        target[pl.ds(to + at, step), :] = unit(source[pl.ds(start + at, step), :])
        return 0

    lax.fori_loop(0, count // step, some, 0)


def products(left, right):
    return lax.dot_general(
        left, right, (((1,), (1,)), ((), ())), preferred_element_type=jnp.float32
    )


def local_kernel(cluster_ref, plan_ref, rows_ref, other_ref, chip_ref, best_ref):
    blocks = rows_ref.shape[0] // BLOCK
    upper, first, theirs = plan_ref[3], plan_ref[4], plan_ref[6]
    wide = 2
    size = wide * BLOCK

    unit_rows(rows_ref, chip_ref, 0, 0, blocks * BLOCK, STEP)

    def normalise_other(turn, _):
        start = pl.multiple_of(turn * size, size)
        to = pl.multiple_of(start + blocks * BLOCK, size)
        unit_rows(other_ref, chip_ref, start, to, size, STEP)
        return 0

    their_from = jnp.where(upper == 1, blocks - theirs, 0)
    their_tiles = lax.div(their_from, wide), lax.div(their_from + theirs + wide - 1, wide)
    lax.fori_loop(their_tiles[0], their_tiles[1], normalise_other, 0)
    best_ref[...] = jnp.full(best_ref.shape, NEVER, jnp.float32)
    other_first = first + blocks - 2 * blocks * upper

    across = blocks // 2

    def tile(turn, _):
        block, left = lax.div(turn, 2) * wide, lax.rem(turn, 2) * across
        here = jnp.where(block < blocks, first + block, other_first + block - blocks)
        same = [
            [cluster_ref[here + i] == cluster_ref[first + left + j] for i in range(wide)]
            for j in range(across)
        ]

        @pl.when(functools.reduce(jnp.logical_or, sum(same, [])))
        def _():
            rows = pl.ds(pl.multiple_of(block * BLOCK, size), size)
            columns = pl.ds(pl.multiple_of(left * BLOCK, across * BLOCK), across * BLOCK)
            product = products(chip_ref[rows, :], chip_ref[columns, :])
            row = lax.broadcasted_iota(jnp.int32, product.shape, 0) + block * BLOCK
            column = lax.broadcasted_iota(jnp.int32, product.shape, 1) + left * BLOCK
            product = jnp.where(row == column, NEVER, product)
            for j in range(across):
                at = pl.ds(left + j, 1)
                best = best_ref[at, :]
                for i in range(wide):
                    piece = product[i * BLOCK : (i + 1) * BLOCK, j * BLOCK : (j + 1) * BLOCK]
                    top = jnp.max(piece, axis=0, keepdims=True)
                    best = jnp.maximum(best, jnp.where(same[j][i], top, NEVER))
                best_ref[at, :] = best

        return 0

    lax.fori_loop(0, 4 * blocks // wide, tile, 0)


def local_best(block_cluster, plan, rows, other):
    blocks = rows.shape[0] // BLOCK
    flops = 4 * rows.shape[0] * rows.shape[0] * rows.shape[1]
    vmem = pl.BlockSpec(memory_space=VMEM)
    return pl.pallas_call(
        local_kernel,
        out_shape=(
            VMEM((2 * rows.shape[0], rows.shape[1]), jnp.bfloat16),
            jax.ShapeDtypeStruct((blocks, BLOCK), jnp.float32),
        ),
        in_specs=[pl.BlockSpec(memory_space=SMEM)] * 2 + [vmem] * 2,
        out_specs=(vmem, vmem),
        compiler_params=pltpu.CompilerParams(vmem_limit_bytes=20 * MIB),
        cost_estimate=pl.CostEstimate(flops=flops, bytes_accessed=8 * rows.size, transcendentals=0),
    )(block_cluster, plan, rows, other)


def cross_kernel(start, tall, wide, whole, plan_ref, got_ref, chip_ref, *refs):
    blocks = chip_ref.shape[0] // BLOCK // 2
    half = 16
    rows, row_best, chip_best = refs[-3:]
    back_ref, near_best_ref, far_best_ref = refs[-6:-3]
    count, near, far, upper = plan_ref[0], plan_ref[1], plan_ref[2], plan_ref[3]
    befores = refs[: len(refs) - 6]
    for ref, before in zip((near_best_ref, far_best_ref, back_ref), befores):
        ref[...] = before[...]
    for ref in (near_best_ref, far_best_ref, back_ref)[len(befores) :]:
        ref[...] = jnp.full(ref.shape, NEVER, jnp.float32)
    got_from = jnp.where(upper == 1, 0, blocks - count)
    got_to = got_from + count
    near_from = jnp.where(upper == 1, blocks - near, 0)
    far_from = blocks + jnp.where(upper == 1, blocks - far, 0)
    near_tile, far_tile = lax.div(near_from, wide), lax.div(far_from, wide)
    near_tiles = lax.div(near_from + near + wide - 1, wide) - near_tile
    far_tiles = lax.div(far_from + far + wide - 1, wide) - far_tile

    def part(step, _):
        first = start + step * tall
        fits_in = [(first + i >= got_from) & (first + i < got_to) for i in range(tall)]

        @pl.when(functools.reduce(jnp.logical_or, fits_in))
        def _():
            at = pl.multiple_of(step * tall * BLOCK, tall * BLOCK)
            unit_rows(got_ref, rows, at, 0, tall * BLOCK, tall * BLOCK if whole else STEP)
            row_best[...] = jnp.full(row_best.shape, NEVER, jnp.float32)

            def tile(turn, _, lowest, wide):
                if whole and wide == blocks:
                    side = chip_ref[: blocks * BLOCK, :]
                else:
                    side = chip_ref[pl.ds(pl.multiple_of(lowest * BLOCK, wide * BLOCK), wide * BLOCK), :]
                product = products(rows[...], side)
                for j in range(wide):
                    block = lowest + j
                    fits = ((block >= near_from) & (block < near_from + near)) | (
                        (block >= far_from) & (block < far_from + far)
                    )
                    best = jnp.full((1, BLOCK), NEVER, jnp.float32)
                    for i in range(tall):
                        at = slice(i * BLOCK, (i + 1) * BLOCK)
                        piece = product[at, j * BLOCK : (j + 1) * BLOCK]
                        row_best[at, :] = jnp.maximum(row_best[at, :], jnp.where(fits, piece, NEVER))
                        top = jnp.max(piece, axis=0, keepdims=True)
                        best = jnp.maximum(best, jnp.where(fits_in[i] & fits, top, NEVER))
                    at = pl.ds(jnp.where(block < blocks, block, block - blocks + half), 1)
                    chip_best[at, :] = jnp.maximum(chip_best[at, :], best)
                return 0

            def one_of_both(turn, _):
                turn = jnp.where(turn < near_tiles, near_tile + turn, far_tile + turn - near_tiles)
                return tile(turn, 0, turn * wide, wide)

            if whole:
                tile(0, 0, 0, blocks)
                lax.fori_loop(far_tile, far_tile + far_tiles, lambda turn, _: tile(turn, 0, turn * wide, wide), 0)
            else:
                lax.fori_loop(0, near_tiles + far_tiles, one_of_both, 0)
            for i in range(tall):
                top = jnp.max(row_best[i * BLOCK : (i + 1) * BLOCK, :].T, axis=0, keepdims=True)
                at = pl.ds(start % BACK_ROWS + step * tall + i, 1)
                back_ref[at, :] = jnp.where(fits_in[i], top, NEVER)

        return 0

    @pl.when(count > 0)
    def _():
        chip_best[...] = jnp.full(chip_best.shape, NEVER, jnp.float32)
        lax.fori_loop(0, got_ref.shape[0] // BLOCK // tall, part, 0)
        near_best_ref[...] = jnp.maximum(near_best_ref[...], chip_best[0:blocks, :])
        far_best_ref[...] = jnp.maximum(far_best_ref[...], chip_best[half : half + blocks, :])


def cross_best(plan, start, got, chip, before, whole):
    blocks = chip.shape[0] // BLOCK // 2
    features = chip.shape[1]
    pieces = got.shape[0] // BLOCK
    tall = max(tall for tall in (1, 2, 3, 4) if pieces % tall == 0)
    out = jax.ShapeDtypeStruct((blocks, BLOCK), jnp.float32)
    vmem = pl.BlockSpec(memory_space=VMEM)
    flops = 2 * got.shape[0] * blocks * BLOCK * features
    return pl.pallas_call(
        functools.partial(cross_kernel, start, tall, 2, whole),
        out_shape=(jax.ShapeDtypeStruct((BACK_ROWS, BLOCK), jnp.float32), out, out),
        in_specs=[pl.BlockSpec(memory_space=SMEM)] + [vmem] * (2 + len(before)),
        out_specs=(vmem, vmem, vmem),
        scratch_shapes=[
            VMEM((tall * BLOCK, features), jnp.bfloat16),
            VMEM((tall * BLOCK, BLOCK), jnp.float32),
            VMEM((32, BLOCK), jnp.float32),
        ],
        compiler_params=pltpu.CompilerParams(vmem_limit_bytes=16 * MIB),
        cost_estimate=pl.CostEstimate(flops=flops, bytes_accessed=4 * got.size, transcendentals=0),
    )(plan, got, chip, *before)


def on_device(embeddings, block_cluster, pair_blocks):
    blocks = embeddings.shape[0] // BLOCK
    devices = lax.axis_size("rows")
    swap = [(i, i ^ 1) for i in range(devices)]
    leftwards = [(i + 1, i) for i in range(1, devices - 1, 2)]
    rightwards = [(b, a) for a, b in leftwards]
    upper = lax.rem(lax.axis_index("rows"), 2)

    other = lax.ppermute(embeddings, "rows", swap)
    way, plan, first, last = make_plan(block_cluster, embeddings, 2 * blocks)

    def send(route, back_route, pieces):
        to_left = route is leftwards

        def branch(embeddings, first, last, other):
            starts = []
            done = 0
            for piece in pieces:
                starts.append(done if to_left else blocks - done - piece)
                done += piece
            got = []
            for start, piece in zip(starts, pieces):
                if piece == LEADING:
                    part = first if to_left else last
                elif 0 <= start < blocks:
                    part = embeddings[start * BLOCK : (start + piece) * BLOCK]
                else:
                    part = other[: piece * BLOCK] if to_left else other[-piece * BLOCK :]
                got.append(lax.ppermute(part, "rows", route))
            chip, best = local_best(block_cluster, plan, embeddings, other)
            found = (best,)
            for start, piece in zip(starts, got):
                back, near, far = cross_best(plan, start, piece, chip, found, piece.shape[0] == 2 * BLOCK and start == starts[-1])
                found = near, far, back
            returned = lax.ppermute(back, "rows", back_route)
            sender = upper == (0 if to_left else 1)
            beyond = sum(pieces) - blocks
            if beyond > 0:
                theirs = returned[blocks : blocks + beyond] if to_left else returned[-beyond:]
                nothing = jnp.full((blocks - beyond, BLOCK), NEVER, jnp.float32)
                theirs = jnp.concatenate([theirs, nothing] if to_left else [nothing, theirs], axis=0)
                far = jnp.where(sender, theirs, far)
            return jnp.maximum(near, jnp.where(sender, returned[:blocks], NEVER)), far

        return branch

    def stay(embeddings, first, last, other):
        _, best = local_best(block_cluster, plan, embeddings, other)
        return best, jnp.full((blocks, BLOCK), NEVER, jnp.float32)

    sends = [send(leftwards, rightwards, pieces) for pieces in PIECES]
    sends += [send(rightwards, leftwards, pieces) for pieces in PIECES]
    best, far_best = lax.switch(way[0], [stay] + sends, embeddings, first, last, other)
    return jnp.maximum(best, lax.ppermute(far_best, "rows", swap)).reshape(-1)


def solution(mesh):
    placed = (P(("groups", "rows"), None), P("groups"), P(("groups", "rows"), None))
    return jax.shard_map(
        on_device, mesh=mesh, in_specs=placed, out_specs=P(("groups", "rows")), check_vma=False
    )
```
